32 devices in a mesh: seq: 32 (over z, y, x, core).
Axes of the slice: x: 2, y: 2, z: 4, core: 2. Of those that a mesh axis runs over, the one named last changes fastest.
Arguments:
- inputs: bfloat16 [32768, 768], P('seq'), may hold values from -6 to 6
- weight_one: bfloat16 [768, 3, 768], P('seq'), may hold values from -0.125 to 0.125
- weight_two: bfloat16 [768, 3, 768], P('seq'), may hold values from -0.125 to 0.125
- cotangent: bfloat16 [32768, 768], P('seq'), may hold values from -6 to 6
Outputs:
- outputs: bfloat16 [32768, 768], P('seq')
- input_grad: bfloat16 [32768, 768], P('seq')
- grad_one: float32 [768, 3, 768], P('seq')
- grad_two: float32 [768, 3, 768], P('seq')
The draws below stay inside these ranges and needn't reach their ends.
All inputs are finite; a program needn't handle non-finite values.
Results may differ from the reference program's by a relative error of at most 0.0056.
Values may be sent and summed in bfloat16 or wider, within the bound.
No kernel may reach another device: no remote copies, remote signals or barrier semaphores. Data moves between devices by JAX's collectives and lax.ppermute only.
A program may use at most 128 MiB of HBM per device.

```python
import math
import jax
import jax.numpy as jnp
from jax import lax

C = 768
TAPS = 3
DILATION_A = 32
DILATION_B = 64
SEQ = 32768


def level_of(key, extent, split, least, high):
    level = 1.0
    for position, blocks in split:
        steps = jax.random.uniform(jax.random.fold_in(jax.random.fold_in(key, 6), position), (blocks,), jnp.float32, least / len(split), high / len(split))
        level = level * jnp.repeat(jnp.exp(steps), extent[position] // blocks).reshape((-1,) + (1,) * (len(extent) - 1 - position))
    return level


def centred(rng, shape, spread, limit, pieces=(), dtype=jnp.bfloat16):
    values = jax.random.normal(rng, shape, jnp.float32) * spread
    if len(pieces) > 0:
        values = level_of(rng, shape, pieces, -0.22, 0.18) * values
    return jnp.clip(values, min=-limit, max=limit).astype(dtype)


def setup_inputs(seed: int = 0) -> dict:
    arg_keys = jax.random.split(jax.random.key(seed), 5)
    return {
        "inputs": centred(arg_keys[0], (SEQ, C), 1.0, 6.0, ((0, 32),)),
        "weight_one": centred(arg_keys[1], (C, TAPS, C), (TAPS * C) ** -0.5, 0.125, ((0, 32),)),
        "weight_two": centred(arg_keys[2], (C, TAPS, C), (TAPS * C) ** -0.5, 0.125, ((0, 32),)),
        "cotangent": centred(arg_keys[3], (SEQ, C), 1.0, 6.0, ((0, 32),)),
    }


def normalize(layer_in):
    residual_in = layer_in.astype(jnp.float32)
    inv_rms = lax.rsqrt(lax.optimization_barrier(jnp.mean(residual_in * residual_in, axis=-1, keepdims=True)) + 1e-06)
    normed = residual_in * inv_rms
    active = (0.5 * normed * (1.0 + jax.scipy.special.erf(normed * 0.7071067811865476))).astype(jnp.bfloat16)
    return (residual_in, normed, inv_rms, active)

def slope_of(normed):
    return 0.5 * (1.0 + jax.scipy.special.erf(normed * 0.7071067811865476)) + normed * jnp.exp(-0.5 * normed * normed) * 0.3989422804014327

def forward_layer(layer_in, weight, spacing):
    residual_in, normed, inv_rms, active = normalize(layer_in)
    padded = jnp.pad(active, ((spacing, spacing), (0, 0)))
    length = layer_in.shape[0]
    mixed = jnp.zeros((length, weight.shape[2]), jnp.float32)
    for tap in range(3):
        mixed = mixed + jnp.dot(padded[tap * spacing:tap * spacing + length], weight[:, tap, :], preferred_element_type=jnp.float32)
    return ((residual_in + mixed).astype(jnp.bfloat16), padded, normed, inv_rms)

def backward_layer(grad_out, padded, normed, inv_rms, weight, spacing, grad_scale):
    length = grad_out.shape[0]
    terms = []
    for tap in range(3):
        terms.append(lax.dot_general(padded[tap * spacing:tap * spacing + length], grad_out, (((0,), (0,)), ((), ())), preferred_element_type=jnp.float32))
    weight_grad = jnp.stack(terms, axis=1) * grad_scale
    grad_pad = jnp.pad(grad_out, ((spacing, spacing), (0, 0)))
    act_grad = jnp.zeros((length, weight.shape[0]), jnp.float32)
    for tap in range(3):
        start_row = (2 - tap) * spacing
        act_grad = act_grad + lax.dot_general(grad_pad[start_row:start_row + length], weight[:, tap, :], (((1,), (1,)), ((), ())), preferred_element_type=jnp.float32)
    norm_grad = act_grad * slope_of(normed)
    passed = grad_out.astype(jnp.float32) + inv_rms * (norm_grad - normed * lax.optimization_barrier(jnp.mean(norm_grad * normed, axis=-1, keepdims=True)))
    return (passed.astype(jnp.bfloat16), weight_grad)

def reference(inputs, weight_one, weight_two, cotangent):
    grad_scale = 1.0 / math.sqrt(inputs.shape[0])
    hidden, pad_one, normed_one, inv_one = forward_layer(inputs, weight_one, DILATION_A)
    outputs, pad_two, normed_two, inv_two = forward_layer(hidden, weight_two, DILATION_B)
    hidden_grad, grad_two = backward_layer(cotangent, pad_two, normed_two, inv_two, weight_two, DILATION_B, grad_scale)
    input_grad, grad_one = backward_layer(hidden_grad, pad_one, normed_one, inv_one, weight_one, DILATION_A, grad_scale)
    return (outputs, input_grad, grad_one, grad_two)
```

```python
import math

import jax
import jax.numpy as jnp
from jax import lax
from jax.sharding import PartitionSpec as P

DILATION_A = 32
DILATION_B = 64
HALO = DILATION_A + DILATION_B


def routes_of(count):
    bits = [1 << k for k in range(count.bit_length() - 2, 0, -1)]
    if len(bits) < 3:
        return [(bits, bits), (bits, bits)]
    far, rest = bits[:1], bits[1:]
    near, middle, last = rest[:-2], rest[-1:], rest[-2:-1]
    first = (far + near + middle + last, far + middle + last + near)
    second = (far + near + last + middle, far + last + middle + near)
    return [first, second]


def step_pairs(count, route, step):
    return [(i, i ^ route[i & 1][step]) for i in range(count)]


def core_pairs(count):
    return [(i, i ^ 1) for i in range(count)]


def relative_channels(count, route, block):
    position = jnp.arange(count * block)
    me = lax.axis_index("seq")
    index, offset = position // block, position % block
    half = count // 2
    other = index // half
    inner = index % half
    core = (me & 1) ^ other
    source = me ^ other
    for step in range(len(route[0])):
        bit = jnp.where(core == 0, route[0][step], route[1][step])
        source = source ^ jnp.where((inner >> step) & 1 == 1, bit, 0)
    return source * block + offset


def one_hot(count, route, block):
    channels = relative_channels(count, route, block)
    rows = lax.broadcasted_iota(jnp.int32, (count * block, count * block), 0)
    return (rows == channels[None, :]).astype(jnp.bfloat16)


def gather_weight(shard, route):
    count = lax.axis_size("seq")
    held = jnp.transpose(shard, (1, 0, 2))
    for step in range(len(route[0])):
        arrived = lax.ppermute(held, "seq", step_pairs(count, route, step))
        held = jnp.concatenate([held, arrived], axis=1)
    other = lax.ppermute(held, "seq", core_pairs(count))
    return jnp.concatenate([held, other], axis=1)


def scatter_grad(term, route, grad_scale):
    count = lax.axis_size("seq")
    half = term.shape[1] // 2
    arrived = lax.ppermute(term[:, half:].astype(jnp.bfloat16), "seq", core_pairs(count))
    held = term[:, :half] + arrived.astype(jnp.float32)
    for step in reversed(range(len(route[0]))):
        half = held.shape[1] // 2
        arrived = lax.ppermute(
            held[:, half:].astype(jnp.bfloat16), "seq", step_pairs(count, route, step)
        )
        held = held[:, :half] + arrived.astype(jnp.float32)
    return jnp.transpose(held * grad_scale, (1, 0, 2))


def permute_channels(values, matrix, dim):
    return lax.dot_general(
        values, matrix, (((1,), (dim,)), ((), ())), preferred_element_type=jnp.float32
    ).astype(jnp.bfloat16)


def normalize(layer_in):
    residual_in = layer_in.astype(jnp.float32)
    inv_rms = lax.rsqrt(jnp.mean(residual_in * residual_in, axis=-1, keepdims=True) + 1e-06)
    normed = residual_in * inv_rms
    active = (0.5 * normed * (1.0 + jax.scipy.special.erf(normed * 0.7071067811865476))).astype(
        jnp.bfloat16
    )
    return normed, inv_rms, active


def slope_of(normed):
    return (
        0.5 * (1.0 + jax.scipy.special.erf(normed * 0.7071067811865476))
        + normed * jnp.exp(-0.5 * normed * normed) * 0.3989422804014327
    )


def mix(active, weight, spacing, length):
    mixed = jnp.zeros((length, weight.shape[2]), jnp.float32)
    for tap in range(3):
        mixed = mixed + jnp.dot(
            active[tap * spacing : tap * spacing + length],
            weight[tap],
            preferred_element_type=jnp.float32,
        )
    return mixed


def weight_term(active, grad_out, spacing):
    length = grad_out.shape[0]
    return jnp.stack(
        [
            lax.dot_general(
                active[tap * spacing : tap * spacing + length],
                grad_out,
                (((0,), (0,)), ((), ())),
                preferred_element_type=jnp.float32,
            )
            for tap in range(3)
        ]
    )


def pass_down(grad_pad, grad_rel, normed, inv_rms, weight, spacing):
    length = grad_rel.shape[0]
    act_grad = jnp.zeros((length, weight.shape[1]), jnp.float32)
    for tap in range(3):
        start_row = (2 - tap) * spacing
        act_grad = act_grad + lax.dot_general(
            grad_pad[start_row : start_row + length],
            weight[tap],
            (((1,), (1,)), ((), ())),
            preferred_element_type=jnp.float32,
        )
    norm_grad = act_grad * slope_of(normed)
    passed = grad_rel.astype(jnp.float32) + inv_rms * (
        norm_grad - normed * jnp.mean(norm_grad * normed, axis=-1, keepdims=True)
    )
    return passed.astype(jnp.bfloat16)


def per_device(inputs, weight_one, weight_two, cotangent):
    count = lax.axis_size("seq")
    me = lax.axis_index("seq")
    length, channels = inputs.shape
    grad_scale = 1.0 / math.sqrt(length * count)
    block = weight_one.shape[0]
    routes = routes_of(count)
    turn_one = one_hot(count, routes[0], block)
    turn_two = one_hot(count, routes[1], block)

    both = jnp.stack([inputs, cotangent])
    forward = [(i, i + 1) for i in range(count - 1)]
    backward = [(i + 1, i) for i in range(count - 1)]
    low = lax.ppermute(both[:, length - HALO :], "seq", forward)
    high = lax.ppermute(both[:, :HALO], "seq", backward)
    wide = jnp.concatenate([low, both, high], axis=1)
    wide_in, wide_cot = wide[0], wide[1]

    def inside(rows, halo):
        position = lax.broadcasted_iota(jnp.int32, (rows, 1), 0) - halo
        return ((position >= 0) | (me > 0)) & ((position < length) | (me < count - 1))

    full_one = gather_weight(weight_one, routes[0])
    full_two = gather_weight(weight_two, routes[1])

    normed_one, inv_one, active_one = normalize(permute_channels(wide_in, turn_one, 0))
    hidden_rows = length + 2 * DILATION_B
    mixed = mix(active_one, full_one, DILATION_A, hidden_rows)
    hidden = (wide_in[DILATION_A : DILATION_A + hidden_rows].astype(jnp.float32) + mixed).astype(
        jnp.bfloat16
    )
    hidden = jnp.where(inside(hidden_rows, DILATION_B), hidden, 0)
    normed_two, inv_two, active_two = normalize(permute_channels(hidden, turn_two, 0))

    grad_two = scatter_grad(weight_term(active_two, cotangent, DILATION_B), routes[1], grad_scale)

    back_rows = length + 2 * DILATION_A
    trim = DILATION_B - DILATION_A
    hidden_grad_rel = pass_down(
        wide_cot,
        permute_channels(wide_cot, turn_two, 0)[DILATION_B : DILATION_B + back_rows],
        normed_two[trim : trim + back_rows],
        inv_two[trim : trim + back_rows],
        full_two,
        DILATION_B,
    )
    hidden_grad = jnp.where(
        inside(back_rows, DILATION_A), permute_channels(hidden_grad_rel, turn_two, 1), 0
    )
    own_grad = hidden_grad[DILATION_A : DILATION_A + length]
    grad_one = scatter_grad(
        weight_term(active_one[DILATION_B : DILATION_B + length + 2 * DILATION_A], own_grad, DILATION_A),
        routes[0],
        grad_scale,
    )
    input_grad_rel = pass_down(
        hidden_grad,
        permute_channels(own_grad, turn_one, 0),
        normed_one[HALO : HALO + length],
        inv_one[HALO : HALO + length],
        full_one,
        DILATION_A,
    )
    input_grad = permute_channels(input_grad_rel, turn_one, 1)
    outputs = (
        hidden[DILATION_B : DILATION_B + length].astype(jnp.float32)
        + mix(active_two, full_two, DILATION_B, length)
    ).astype(jnp.bfloat16)
    return (outputs, input_grad, grad_one, grad_two)


def solution(mesh):
    in_specs = (P("seq", None), P("seq", None, None), P("seq", None, None), P("seq", None))
    out_specs = (P("seq", None), P("seq", None), P("seq", None, None), P("seq", None, None))
    return jax.shard_map(
        per_device, mesh=mesh, in_specs=in_specs, out_specs=out_specs, check_vma=False
    )
```

```python
import math

import jax
import jax.numpy as jnp
from jax import lax
from jax.sharding import PartitionSpec as P

DILATION_A = 32
DILATION_B = 64
HALO = DILATION_A + DILATION_B


def routes_of(count):
    bits = [1 << k for k in range(count.bit_length() - 2, 0, -1)]
    far, rest = bits[:1], bits[1:]
    turn = [k % max(len(rest), 1) for k in range(3)]
    return [far + rest[k:] + rest[:k] for k in turn]


def partners(count, bit):
    return [(i, i ^ bit) for i in range(count)]


def one_hot(count, block):
    position = jnp.arange(count * block)
    index, offset = position // block, position % block
    half = count // 2
    source = lax.axis_index("seq") ^ (2 * (index % half) + index // half)
    rows = lax.broadcasted_iota(jnp.int32, (count * block, count * block), 0)
    return (rows == (source * block + offset)[None, :]).astype(jnp.bfloat16)


def gather_steps(shards, routes):
    count = lax.axis_size("seq")
    held = [(shard, ()) for shard in shards]
    for step in range(len(routes[0])):
        arrived = [
            lax.ppermute(block, "seq", partners(count, route[step]))
            for (block, _), route in zip(held, routes)
        ]
        yield arrived
        joined = []
        for (block, bits), new, route in zip(held, arrived, routes):
            bits = tuple(sorted(bits + (route[step],), reverse=True))
            joined.append((jnp.stack([block, new], axis=bits.index(route[step])), bits))
        held = joined
    flat = [block.reshape(-1, block.shape[-1]) for block, _ in held]
    other = [lax.ppermute(block, "seq", partners(count, 1)) for block in flat]
    yield other
    return [jnp.concatenate(pair, axis=0) for pair in zip(flat, other)]


def gather_weights(shard_one, shard_two, routes):
    first = gather_steps([shard_one[:, tap, :] for tap in range(3)], routes)
    arrived = next(first)
    shards = [shard_two[:, tap, :] for tap in range(3)]
    shards = lax.optimization_barrier(tuple(shards) + tuple(arrived))[:3]
    full = [run_out(first), run_out(gather_steps(list(shards), routes))]
    return full


def run_out(steps):
    while True:
        try:
            next(steps)
        except StopIteration as end:
            return end.value


def scatter_tap(term, route, block, grad_scale):
    count = lax.axis_size("seq")
    half = term.shape[0] // 2
    arrived = lax.ppermute(term[half:].astype(jnp.bfloat16), "seq", partners(count, 1))
    held = term[:half] + arrived.astype(jnp.float32)
    bits = sorted(route, reverse=True)
    held = held.reshape((2,) * len(bits) + (block, term.shape[1]))
    for bit in reversed(route):
        axis = bits.index(bit)
        bits.remove(bit)
        keep, send = (lax.index_in_dim(held, side, axis, keepdims=False) for side in range(2))
        arrived = lax.ppermute(send.astype(jnp.bfloat16), "seq", partners(count, bit))
        held = keep + arrived.astype(jnp.float32)
    return held * grad_scale


def scatter_grad(terms, routes, block, grad_scale):
    return jnp.stack(
        [scatter_tap(term, route, block, grad_scale) for term, route in zip(terms, routes)], axis=1
    )


def permute_channels(values, matrix, dim):
    return lax.dot_general(
        values, matrix, (((1,), (dim,)), ((), ())), preferred_element_type=jnp.float32
    ).astype(jnp.bfloat16)


def normalize(layer_in):
    residual_in = layer_in.astype(jnp.float32)
    inv_rms = lax.rsqrt(jnp.mean(residual_in * residual_in, axis=-1, keepdims=True) + 1e-06)
    normed = residual_in * inv_rms
    active = (0.5 * normed * (1.0 + jax.scipy.special.erf(normed * 0.7071067811865476))).astype(
        jnp.bfloat16
    )
    return normed, inv_rms, active


def slope_of(normed):
    return (
        0.5 * (1.0 + jax.scipy.special.erf(normed * 0.7071067811865476))
        + normed * jnp.exp(-0.5 * normed * normed) * 0.3989422804014327
    )


def mix(active, weight, spacing, length):
    mixed = jnp.zeros((length, weight[0].shape[1]), jnp.float32)
    for tap in range(3):
        mixed = mixed + jnp.dot(
            active[tap * spacing : tap * spacing + length],
            weight[tap],
            preferred_element_type=jnp.float32,
        )
    return mixed


def weight_term(active, grad_out, spacing):
    length = grad_out.shape[0]
    return [
        lax.dot_general(
            active[tap * spacing : tap * spacing + length],
            grad_out,
            (((0,), (0,)), ((), ())),
            preferred_element_type=jnp.float32,
        )
        for tap in range(3)
    ]


def pass_down(grad_pad, grad_rel, normed, inv_rms, weight, spacing):
    length = grad_rel.shape[0]
    act_grad = jnp.zeros((length, weight[0].shape[0]), jnp.float32)
    for tap in range(3):
        start_row = (2 - tap) * spacing
        act_grad = act_grad + lax.dot_general(
            grad_pad[start_row : start_row + length],
            weight[tap],
            (((1,), (1,)), ((), ())),
            preferred_element_type=jnp.float32,
        )
    norm_grad = act_grad * slope_of(normed)
    passed = grad_rel.astype(jnp.float32) + inv_rms * (
        norm_grad - normed * jnp.mean(norm_grad * normed, axis=-1, keepdims=True)
    )
    return passed.astype(jnp.bfloat16)


def per_device(inputs, weight_one, weight_two, cotangent):
    count = lax.axis_size("seq")
    me = lax.axis_index("seq")
    length, channels = inputs.shape
    grad_scale = 1.0 / math.sqrt(length * count)
    block = weight_one.shape[0]
    routes = routes_of(count)
    turn = one_hot(count, block)

    forward = [(i, i + 1) for i in range(count - 1)]
    backward = [(i + 1, i) for i in range(count - 1)]
    low = lax.ppermute(
        jnp.concatenate([inputs[length - HALO :], cotangent[length - HALO :]]), "seq", forward
    )
    high = lax.ppermute(jnp.concatenate([inputs[:HALO], cotangent[:HALO]]), "seq", backward)
    wide_in = jnp.concatenate([low[:HALO], inputs, high[:HALO]])
    wide_cot = jnp.concatenate([low[HALO:], cotangent, high[HALO:]])

    def inside(rows, halo):
        position = lax.broadcasted_iota(jnp.int32, (rows, 1), 0) - halo
        return ((position >= 0) | (me > 0)) & ((position < length) | (me < count - 1))

    full_one, full_two = gather_weights(weight_one, weight_two, routes)

    normed_one, inv_one, active_one = normalize(permute_channels(wide_in, turn, 0))
    hidden_rows = length + 2 * DILATION_B
    mixed = mix(active_one, full_one, DILATION_A, hidden_rows)
    hidden = (wide_in[DILATION_A : DILATION_A + hidden_rows].astype(jnp.float32) + mixed).astype(
        jnp.bfloat16
    )
    hidden = jnp.where(inside(hidden_rows, DILATION_B), hidden, 0)
    normed_two, inv_two, active_two = normalize(permute_channels(hidden, turn, 0))

    grad_two = scatter_grad(weight_term(active_two, cotangent, DILATION_B), routes, block, grad_scale)

    back_rows = length + 2 * DILATION_A
    trim = DILATION_B - DILATION_A
    hidden_grad_rel = pass_down(
        wide_cot,
        permute_channels(wide_cot, turn, 0)[DILATION_B : DILATION_B + back_rows],
        normed_two[trim : trim + back_rows],
        inv_two[trim : trim + back_rows],
        full_two,
        DILATION_B,
    )
    hidden_grad = jnp.where(
        inside(back_rows, DILATION_A), permute_channels(hidden_grad_rel, turn, 1), 0
    )
    own_grad = hidden_grad[DILATION_A : DILATION_A + length]
    grad_one = scatter_grad(
        weight_term(active_one[DILATION_B : DILATION_B + length + 2 * DILATION_A], own_grad, DILATION_A),
        routes,
        block,
        grad_scale,
    )
    input_grad_rel = pass_down(
        hidden_grad,
        permute_channels(own_grad, turn, 0),
        normed_one[HALO : HALO + length],
        inv_one[HALO : HALO + length],
        full_one,
        DILATION_A,
    )
    input_grad = permute_channels(input_grad_rel, turn, 1)
    outputs = (
        hidden[DILATION_B : DILATION_B + length].astype(jnp.float32)
        + mix(active_two, full_two, DILATION_B, length)
    ).astype(jnp.bfloat16)
    return (outputs, input_grad, grad_one, grad_two)


def solution(mesh):
    in_specs = (P("seq", None), P("seq", None, None), P("seq", None, None), P("seq", None))
    out_specs = (P("seq", None), P("seq", None), P("seq", None, None), P("seq", None, None))
    return jax.shard_map(
        per_device, mesh=mesh, in_specs=in_specs, out_specs=out_specs, check_vma=False
    )
```

```python
import math

import jax
import jax.numpy as jnp
from jax import lax
from jax.experimental import pallas as pl
from jax.experimental.pallas import tpu as pltpu
from jax.sharding import PartitionSpec as P

DILATION_A = 32
DILATION_B = 64
HALO = DILATION_A + DILATION_B


def routes_of(count):
    bits = [1 << k for k in range(count.bit_length() - 2, 0, -1)]
    if len(bits) < 4:
        return [(bits, bits), (bits, bits)]
    far, (depth, row, column) = bits[:-3], bits[-3:]
    first = (far + [depth, column, row], far + [column, row, depth])
    second = (far + [depth, column, row], far + [row, column, depth])
    return [first, second]


def step_pairs(count, route, step):
    return [(i, i ^ route[i & 1][step]) for i in range(count)]


def core_pairs(count):
    return [(i, i ^ 1) for i in range(count)]


def relative_channels(count, route, block):
    position = jnp.arange(count * block)
    me = lax.axis_index("seq")
    index, offset = position // block, position % block
    half = count // 2
    other = index // half
    inner = index % half
    core = (me & 1) ^ other
    source = me ^ other
    for step in range(len(route[0])):
        bit = jnp.where(core == 0, route[0][step], route[1][step])
        source = source ^ jnp.where((inner >> step) & 1 == 1, bit, 0)
    return source * block + offset


def one_hot(count, route, block):
    channels = relative_channels(count, route, block)
    rows = lax.broadcasted_iota(jnp.int32, (count * block, count * block), 0)
    return (rows == channels[None, :]).astype(jnp.bfloat16)


def after(value, *others):
    return lax.optimization_barrier((value,) + others)[0]


class Gather:
    def __init__(self, shard, route):
        self.held = jnp.transpose(shard, (1, 0, 2))
        self.route = route
        self.steps = len(route[0])
        self.step = 0
        self.pieces = []

    def send(self):
        count = lax.axis_size("seq")
        if self.step < self.steps:
            self.arrived = lax.ppermute(self.held, "seq", step_pairs(count, self.route, self.step))
        if self.step >= self.steps - 1:
            self.pieces.append((self.held, lax.ppermute(self.held, "seq", core_pairs(count))))
        self.step += 1

    def join(self, *others):
        arrived = after(self.arrived, *others)
        if self.step < self.steps:
            arrived = jnp.concatenate([self.held, arrived], axis=1)
        self.held = lax.optimization_barrier(arrived)
        return self.held

    def full(self):
        own, other = zip(*self.pieces)
        return own + other


class Scatter:
    def __init__(self, sends, route):
        self.route = route
        self.left = list(reversed(range(len(route[0]))))
        pairs = core_pairs(lax.axis_size("seq"))
        self.arrived = [lax.ppermute(send, "seq", pairs) for send in sends]

    def keep(self, keep):
        self.kept = keep

    def add(self, *others):
        arrived = self.arrived
        if isinstance(arrived, list):
            arrived = jnp.stack(lax.optimization_barrier(tuple(arrived) + others)[:3])
        else:
            arrived = after(arrived, *others)
        half = self.kept.shape[1] // 2
        send = (self.kept[:, half:] + arrived[:, half:].astype(jnp.float32)).astype(jnp.bfloat16)
        keep = self.kept[:, :half] + arrived[:, :half].astype(jnp.float32)
        send, self.kept = lax.optimization_barrier((send, keep))
        pairs = step_pairs(lax.axis_size("seq"), self.route, self.left.pop(0))
        self.arrived = lax.ppermute(send, "seq", pairs)
        return send

    def finish(self, grad_scale):
        return jnp.transpose((self.kept + self.arrived.astype(jnp.float32)) * grad_scale, (1, 0, 2))


def permute_channels(values, matrix, dim):
    return lax.dot_general(
        values, matrix, (((1,), (dim,)), ((), ())), preferred_element_type=jnp.float32
    ).astype(jnp.bfloat16)


CHUNK = 16
BLOCKS = 4
FREE = pl.CostEstimate(flops=0, bytes_accessed=0, transcendentals=0)


def on_chip(*arrays):
    return [pltpu.with_memory_space_constraint(array, pltpu.VMEM) for array in arrays]


def call(kernel, name, arrays, outs, scratch=(), edges=None, room=8):
    scalars = [] if edges is None else [edges]
    return pl.pallas_call(
        kernel,
        in_specs=[pl.BlockSpec(memory_space=pltpu.SMEM)] * len(scalars)
        + [pl.BlockSpec(memory_space=pltpu.VMEM)] * len(arrays),
        out_specs=[pl.BlockSpec(memory_space=pltpu.VMEM)] * len(outs),
        out_shape=[pltpu.VMEM(shape, dtype) for shape, dtype in outs],
        scratch_shapes=list(scratch),
        compiler_params=pltpu.CompilerParams(vmem_limit_bytes=room * 2**20),
        cost_estimate=FREE,
        name=name,
    )(*scalars, *on_chip(*arrays))


def blocks_of(rows):
    step = rows // BLOCKS
    return [(first, step) for first in range(0, rows, step)]


def parts(first, rows):
    return [slice(start, start + CHUNK) for start in range(first, first + rows, CHUNK)]


def inverse_rms(values):
    return lax.rsqrt(jnp.mean(values * values, axis=-1, keepdims=True) + 1e-06)


def cumulative_of(normed):
    return 0.5 * (1.0 + lax.erf(normed * 0.7071067811865476))


def activate(part, target, rel_ref, active_ref):
    values = rel_ref[part].astype(jnp.float32)
    normed = values * inverse_rms(values)
    active_ref[target] = (normed * cumulative_of(normed)).astype(jnp.bfloat16)


def inside(edge_ref, first, rows):
    row = first + lax.broadcasted_iota(jnp.int32, (rows, 1), 0)
    return (row >= edge_ref[0]) & (row < edge_ref[1])


def active_kernel(layer_in_ref, grad_ref, turn_ref, next_turn_ref, active_ref, grad_rel_ref, rel_ref, *, offset):
    for first, rows in blocks_of(layer_in_ref.shape[0]):
        block = slice(first, first + rows)
        rel_ref[:rows] = jnp.dot(
            layer_in_ref[block], turn_ref[...], preferred_element_type=jnp.float32
        ).astype(jnp.bfloat16)
        for part in parts(0, rows):
            activate(part, slice(first + part.start, first + part.stop), rel_ref, active_ref)
    for first, rows in blocks_of(grad_rel_ref.shape[0]):
        grad_rel_ref[first : first + rows] = jnp.dot(
            grad_ref[offset + first : offset + first + rows],
            next_turn_ref[...],
            preferred_element_type=jnp.float32,
        ).astype(jnp.bfloat16)


def first_active(layer_in, grad, turn, next_turn, offset, length):
    rows, channels = layer_in.shape
    return call(
        lambda *refs: active_kernel(*refs, offset=offset),
        "first_active",
        [layer_in, grad, turn, next_turn],
        [((rows, channels), jnp.bfloat16), ((length, channels), jnp.bfloat16)],
        [pltpu.VMEM((rows // BLOCKS, channels), jnp.bfloat16)],
        room=6,
    )


def layer_kernel(edge_ref, *refs, spacing, offset, follow):
    pieces, (active_ref, layer_in_ref, *refs) = refs[:4], refs[4:]
    if follow:
        turn_ref, out_ref, rel_ref, next_ref, weight = refs
    else:
        out_ref, weight = refs
    length, channels = out_ref.shape
    size = channels // 4
    for tap in range(3):
        for index, piece in enumerate(pieces):
            first = tap * channels + index * size
            weight[first : first + size] = piece[tap]
    for first, rows in blocks_of(length):
        block = slice(first, first + rows)
        windows = [
            active_ref[first + tap * spacing : first + tap * spacing + rows] for tap in range(3)
        ]
        mixed = jnp.dot(
            jnp.concatenate(windows, axis=1), weight[...], preferred_element_type=jnp.float32
        )
        out = layer_in_ref[offset + first : offset + first + rows].astype(jnp.float32) + mixed
        if follow:
            out = jnp.where(inside(edge_ref, first, rows), out, 0.0)
        out_ref[block] = out.astype(jnp.bfloat16)
        if follow:
            rel_ref[block] = jnp.dot(
                out_ref[block], turn_ref[...], preferred_element_type=jnp.float32
            ).astype(jnp.bfloat16)
            for part in parts(first, rows):
                activate(part, part, rel_ref, next_ref)


def layer(edges, pieces, active, layer_in, offset, length, spacing, turn=None):
    channels = active.shape[1]
    follow = turn is not None
    shape = (length, channels)
    outs = [(shape, jnp.bfloat16)]
    if follow:
        outs += [(shape, jnp.bfloat16)] * 2
    return call(
        lambda *refs: layer_kernel(*refs, spacing=spacing, offset=offset, follow=follow),
        "layer",
        [*pieces, active, layer_in] + ([turn] if follow else []),
        outs,
        [pltpu.VMEM((3 * channels, channels), jnp.bfloat16)],
        edges,
    )


def weight_kernel(active_ref, grad_ref, *outs, spacing, offset, halo, side):
    channels = active_ref.shape[1]
    length = grad_ref.shape[0] - 2 * halo
    half = channels // 2
    turned = active_ref[offset : offset + length, side * half : (side + 1) * half].T
    for tap in range(3):
        first = halo + (1 - tap) * spacing
        term = jnp.dot(
            turned, grad_ref[first : first + length], preferred_element_type=jnp.float32
        )
        if len(outs) == 3:
            outs[tap][...] = term.astype(jnp.bfloat16)
        else:
            outs[0][tap] = term


def weight_term(active, offset, grad_wide, side, spacing, halo):
    channels = active.shape[1]
    half = channels // 2
    if side == 0:
        outs = [((3, half, channels), jnp.float32)]
    else:
        outs = [((half, channels), jnp.bfloat16)] * 3
    out = call(
        lambda *refs: weight_kernel(*refs, spacing=spacing, offset=offset, halo=halo, side=side),
        "weight_term",
        [active, grad_wide],
        outs,
    )
    return out[0] if side == 0 else out


def pass_kernel(edge_ref, *refs, spacing, offset):
    pieces, refs = refs[:4], refs[4:]
    grad_ref, grad_rel_ref, layer_in_ref, turn_ref, out_ref, rel_ref, weight, act_grad = refs
    length, channels = out_ref.shape
    size = channels // 4
    for tap in range(3):
        for index, piece in enumerate(pieces):
            weight[index * size : (index + 1) * size, tap * channels : (tap + 1) * channels] = piece[tap]
    for first, rows in blocks_of(length):
        windows = [
            grad_ref[first + (2 - tap) * spacing : first + (2 - tap) * spacing + rows]
            for tap in range(3)
        ]
        act_grad[...] = lax.dot_general(
            jnp.concatenate(windows, axis=1),
            weight[...],
            (((1,), (1,)), ((), ())),
            preferred_element_type=jnp.float32,
        )
        for part in parts(first, rows):
            source = slice(offset + part.start, offset + part.stop)
            values = layer_in_ref[source].astype(jnp.float32)
            inv_rms = inverse_rms(values)
            normed = values * inv_rms
            slope = (
                cumulative_of(normed)
                + normed * jnp.exp(-0.5 * normed * normed) * 0.3989422804014327
            )
            norm_grad = act_grad[part.start - first : part.stop - first] * slope
            passed = grad_rel_ref[part].astype(jnp.float32) + inv_rms * (
                norm_grad - normed * jnp.mean(norm_grad * normed, axis=-1, keepdims=True)
            )
            passed = jnp.where(inside(edge_ref, part.start, CHUNK), passed, 0.0)
            rel_ref[part] = passed.astype(jnp.bfloat16)
        block = slice(first, first + rows)
        out_ref[block] = lax.dot_general(
            rel_ref[block], turn_ref[...], (((1,), (1,)), ((), ())), preferred_element_type=jnp.float32
        ).astype(jnp.bfloat16)


def pass_down(edges, pieces, grad_pad, grad_rel, layer_in, offset, turn, spacing):
    length = grad_pad.shape[0] - 2 * spacing
    channels = layer_in.shape[1]
    shape = (length, channels)
    return call(
        lambda *refs: pass_kernel(*refs, spacing=spacing, offset=offset),
        "pass_down",
        [*pieces, grad_pad, grad_rel, layer_in, turn],
        [(shape, jnp.bfloat16)],
        [
            pltpu.VMEM(shape, jnp.bfloat16),
            pltpu.VMEM((channels, 3 * channels), jnp.bfloat16),
            pltpu.VMEM((length // BLOCKS, channels), jnp.float32),
        ],
        edges,
    )[0]


def per_device(inputs, weight_one, weight_two, cotangent):
    count = lax.axis_size("seq")
    me = lax.axis_index("seq")
    length, channels = inputs.shape
    grad_scale = 1.0 / math.sqrt(length * count)
    block = weight_one.shape[0]
    routes = routes_of(count)
    turn_one = one_hot(count, routes[0], block)
    turn_two = one_hot(count, routes[1], block)

    back_rows = length + 2 * DILATION_A
    hidden_rows = length + 2 * DILATION_B

    def edges_of(rows, halo):
        first = jnp.where(me > 0, 0, halo)
        last = jnp.where(me < count - 1, rows, rows - halo)
        return jnp.stack([first, last]).astype(jnp.int32)

    one, two = Gather(weight_one, routes[0]), Gather(weight_two, routes[1])

    def gather_both(*others):
        joined = two.join(*others)
        joined = one.join(joined)
        one.send()
        two.send()
        return joined

    one.send()
    edges_low = jnp.concatenate([inputs[:HALO], cotangent[:HALO]])
    edges_high = jnp.concatenate([inputs[length - HALO :], cotangent[length - HALO :]])
    odd = (me & 1) == 1
    inner = jnp.where(odd, edges_low, edges_high)
    outer = jnp.where(odd, edges_high, edges_low)
    joined = one.join(inner, outer)
    one.send()
    two.held = after(two.held, joined)
    two.send()
    joined = one.join()
    one.send()
    joined = two.join(joined)
    two.send()
    for _ in range(one.steps - 3):
        joined = gather_both()
    across = [(i, i + 1) for i in range(1, count - 1, 2)] + [(i + 1, i) for i in range(1, count - 1, 2)]
    inner = lax.ppermute(after(inner, joined), "seq", core_pairs(count))
    outer = lax.ppermute(after(outer, joined), "seq", across)
    low = jnp.where(odd, inner, outer)
    high = jnp.where(odd, outer, inner)
    wide_in = jnp.concatenate([low[:HALO], inputs, high[:HALO]])
    wide_cot = jnp.concatenate([low[HALO:], cotangent, high[HALO:]])
    active_one, cot_rel = first_active(wide_in, wide_cot, turn_one, turn_two, DILATION_B, back_rows)
    joined = gather_both(cot_rel)
    full_one = one.full()

    hidden, rel_two, active_two = layer(
        edges_of(hidden_rows, DILATION_B),
        full_one,
        after(active_one, joined),
        wide_in,
        DILATION_A,
        hidden_rows,
        DILATION_A,
        turn_two,
    )
    send_two = weight_term(active_two, DILATION_B, wide_cot, 1, DILATION_B, HALO)
    scatter_two = Scatter(send_two, routes[1])
    joined = two.join(*send_two)
    two.send()
    full_two = two.full()
    scatter_two.keep(
        weight_term(active_two, DILATION_B, after(wide_cot, joined), 0, DILATION_B, HALO)
    )
    sent = scatter_two.add()

    wide_grad = pass_down(
        edges_of(back_rows, DILATION_A),
        full_two,
        after(wide_cot, sent),
        cot_rel,
        rel_two,
        DILATION_B - DILATION_A,
        turn_two,
        DILATION_B,
    )

    send_one = weight_term(active_one, HALO, wide_grad, 1, DILATION_A, DILATION_A)
    scatter_one = Scatter(send_one, routes[0])
    keep_one = weight_term(active_one, HALO, after(wide_grad, *send_one), 0, DILATION_A, DILATION_A)
    scatter_one.keep(keep_one)
    sent = scatter_two.add(keep_one)
    sent = scatter_one.add(sent)
    own_rel = permute_channels(after(wide_grad, sent)[DILATION_A : DILATION_A + length], turn_one, 0)
    input_grad = pass_down(
        edges_of(length, 0),
        full_one,
        wide_grad,
        own_rel,
        permute_channels(after(inputs, sent), turn_one, 0),
        0,
        turn_one,
        DILATION_A,
    )
    sent = scatter_two.add(input_grad)
    sent = scatter_one.add(sent)
    (outputs,) = layer(
        edges_of(length, 0),
        full_two,
        after(active_two, sent),
        hidden,
        DILATION_B,
        length,
        DILATION_B,
    )
    rest = [outputs]
    while scatter_one.left:
        if scatter_two.left:
            rest = [scatter_two.add(*rest)]
        rest = [scatter_one.add(*rest)]
    grad_one = scatter_one.finish(grad_scale)
    grad_two = scatter_two.finish(grad_scale)
    return (outputs, input_grad, grad_one, grad_two)


def solution(mesh):
    in_specs = (P("seq", None), P("seq", None, None), P("seq", None, None), P("seq", None))
    out_specs = (P("seq", None), P("seq", None), P("seq", None, None), P("seq", None, None))
    return jax.shard_map(
        per_device, mesh=mesh, in_specs=in_specs, out_specs=out_specs, check_vma=False
    )
```

```python
import math

import jax
import jax.numpy as jnp
from jax import lax
from jax.experimental import pallas as pl
from jax.experimental.pallas import tpu as pltpu
from jax.sharding import PartitionSpec as P

DILATION_A = 32
DILATION_B = 64
HALO = DILATION_A + DILATION_B


def routes_of(count):
    bits = [1 << k for k in range(count.bit_length() - 2, 0, -1)]
    if len(bits) < 4:
        return [(bits, bits), (bits, bits)]
    far, (depth, row, column) = bits[:-3], bits[-3:]
    first = (far + [depth, column, row], far + [column, row, depth])
    second = (far + [depth, column, row], far + [row, column, depth])
    return [first, second]


def step_pairs(count, route, step):
    return [(i, i ^ route[i & 1][step]) for i in range(count)]


def core_pairs(count):
    return [(i, i ^ 1) for i in range(count)]


def relative_channels(count, route, block):
    position = jnp.arange(count * block)
    me = lax.axis_index("seq")
    index, offset = position // block, position % block
    half = count // 2
    other = index // half
    inner = index % half
    core = (me & 1) ^ other
    source = me ^ other
    for step in range(len(route[0])):
        bit = jnp.where(core == 0, route[0][step], route[1][step])
        source = source ^ jnp.where((inner >> step) & 1 == 1, bit, 0)
    return source * block + offset


def one_hot(count, route, block):
    channels = relative_channels(count, route, block)
    rows = lax.broadcasted_iota(jnp.int32, (count * block, count * block), 0)
    return (rows == channels[None, :]).astype(jnp.bfloat16)


def after(value, *others):
    return lax.optimization_barrier((value,) + others)[0]


class Gather:
    def __init__(self, shard, route):
        self.held = jnp.transpose(shard, (1, 0, 2))
        self.route = route
        self.steps = len(route[0])
        self.step = 0
        self.pieces = []

    def send(self):
        count = lax.axis_size("seq")
        if self.step < self.steps:
            self.arrived = lax.ppermute(self.held, "seq", step_pairs(count, self.route, self.step))
        if self.step >= self.steps - 1:
            self.pieces.append((self.held, lax.ppermute(self.held, "seq", core_pairs(count))))
        self.step += 1

    def join(self, *others):
        arrived = after(self.arrived, *others)
        if self.step < self.steps:
            arrived = join_rows(self.held, arrived)
        self.held = lax.optimization_barrier(arrived)
        return self.held

    def full(self):
        own, other = zip(*self.pieces)
        return own + other


class Scatter:
    def __init__(self, sends, route):
        self.route = route
        self.left = list(reversed(range(len(route[0]))))
        pairs = core_pairs(lax.axis_size("seq"))
        self.arrived = [lax.ppermute(send, "seq", pairs) for send in sends]

    def keep(self, keep):
        self.kept = keep

    def add(self, *others):
        arrived = self.arrived
        if isinstance(arrived, list):
            arrived = jnp.stack(lax.optimization_barrier(tuple(arrived) + others)[:3])
        else:
            arrived = after(arrived, *others)
        half = self.kept.shape[1] // 2
        send = (self.kept[:, half:] + arrived[:, half:].astype(jnp.float32)).astype(jnp.bfloat16)
        keep = self.kept[:, :half] + arrived[:, :half].astype(jnp.float32)
        send, self.kept = lax.optimization_barrier((send, keep))
        pairs = step_pairs(lax.axis_size("seq"), self.route, self.left.pop(0))
        self.arrived = lax.ppermute(send, "seq", pairs)
        return send

    def finish(self, grad_scale):
        return jnp.transpose((self.kept + self.arrived.astype(jnp.float32)) * grad_scale, (1, 0, 2))


def permute_channels(values, matrix, dim):
    return lax.dot_general(
        values, matrix, (((1,), (dim,)), ((), ())), preferred_element_type=jnp.float32
    ).astype(jnp.bfloat16)


CHUNK = 16
BLOCKS = 4
FREE = pl.CostEstimate(flops=0, bytes_accessed=0, transcendentals=0)


def on_chip(*arrays):
    return [pltpu.with_memory_space_constraint(array, pltpu.VMEM) for array in arrays]


def call(kernel, name, arrays, outs, scratch=(), edges=None, room=8):
    scalars = [] if edges is None else [edges]
    return pl.pallas_call(
        kernel,
        in_specs=[pl.BlockSpec(memory_space=pltpu.SMEM)] * len(scalars)
        + [pl.BlockSpec(memory_space=pltpu.VMEM)] * len(arrays),
        out_specs=[pl.BlockSpec(memory_space=pltpu.VMEM)] * len(outs),
        out_shape=[pltpu.VMEM(shape, dtype) for shape, dtype in outs],
        scratch_shapes=list(scratch),
        compiler_params=pltpu.CompilerParams(vmem_limit_bytes=room * 2**20),
        cost_estimate=FREE,
        name=name,
    )(*scalars, *on_chip(*arrays))


def blocks_of(rows):
    step = rows // BLOCKS
    return [(first, step) for first in range(0, rows, step)]


def parts(first, rows):
    return [slice(start, start + CHUNK) for start in range(first, first + rows, CHUNK)]


def inverse_rms(values):
    return lax.rsqrt(jnp.mean(values * values, axis=-1, keepdims=True) + 1e-06)


def cumulative_of(normed):
    return 0.5 * (1.0 + lax.erf(normed * 0.7071067811865476))


def activate(part, target, rel_ref, active_ref):
    values = rel_ref[part].astype(jnp.float32)
    normed = values * inverse_rms(values)
    active_ref[target] = (normed * cumulative_of(normed)).astype(jnp.bfloat16)


def inside(edge_ref, first, rows):
    row = first + lax.broadcasted_iota(jnp.int32, (rows, 1), 0)
    return (row >= edge_ref[0]) & (row < edge_ref[1])


def join_kernel(first_ref, second_ref, out_ref):
    rows = first_ref.shape[1]
    out_ref[:, :rows] = first_ref[...]
    out_ref[:, rows:] = second_ref[...]


def join_rows(first, second):
    taps, rows, channels = first.shape
    if rows % 16:
        return jnp.concatenate([first, second], axis=1)
    shape = (taps, 2 * rows, channels)
    return call(join_kernel, "join_rows", [first, second], [(shape, first.dtype)], room=4)[0]


def active_kernel(
    odd_ref, layer_in_ref, grad_ref, inner_ref, outer_ref, turn_ref, next_turn_ref,
    wide_in_ref, wide_grad_ref, active_ref, grad_rel_ref, rel_ref, *, offset
):
    length = layer_in_ref.shape[0]
    halo = inner_ref.shape[0] // 2
    odd = odd_ref[0] == 1
    for index, (wide_ref, own_ref) in enumerate(((wide_in_ref, layer_in_ref), (wide_grad_ref, grad_ref))):
        rows = slice(index * halo, (index + 1) * halo)
        wide_ref[:halo] = jnp.where(odd, inner_ref[rows], outer_ref[rows])
        wide_ref[halo : halo + length] = own_ref[...]
        wide_ref[halo + length :] = jnp.where(odd, outer_ref[rows], inner_ref[rows])
    for first, rows in blocks_of(wide_in_ref.shape[0]):
        rel_ref[...] = jnp.dot(
            wide_in_ref[first : first + rows], turn_ref[...], preferred_element_type=jnp.float32
        ).astype(jnp.bfloat16)
        for part in parts(0, rows):
            activate(part, slice(first + part.start, first + part.stop), rel_ref, active_ref)
    for first, rows in blocks_of(grad_rel_ref.shape[0]):
        grad_rel_ref[first : first + rows] = jnp.dot(
            wide_grad_ref[offset + first : offset + first + rows],
            next_turn_ref[...],
            preferred_element_type=jnp.float32,
        ).astype(jnp.bfloat16)


def first_active(odd, layer_in, grad, inner, outer, turn, next_turn, offset, back_rows):
    length, channels = layer_in.shape
    rows = length + inner.shape[0]
    wide = ((rows, channels), jnp.bfloat16)
    return call(
        lambda *refs: active_kernel(*refs, offset=offset),
        "first_active",
        [layer_in, grad, inner, outer, turn, next_turn],
        [wide, wide, wide, ((back_rows, channels), jnp.bfloat16)],
        [pltpu.VMEM((rows // BLOCKS, channels), jnp.bfloat16)],
        odd,
        room=6,
    )


def layer_kernel(edge_ref, *refs, spacing, offset, follow):
    pieces, (active_ref, layer_in_ref, *refs) = refs[:4], refs[4:]
    if follow:
        turn_ref, out_ref, rel_ref, next_ref, weight = refs
    else:
        out_ref, weight = refs
    length, channels = out_ref.shape
    size = channels // 4
    for tap in range(3):
        for index, piece in enumerate(pieces):
            first = tap * channels + index * size
            weight[first : first + size] = piece[tap]
    for first, rows in blocks_of(length):
        block = slice(first, first + rows)
        windows = [
            active_ref[first + tap * spacing : first + tap * spacing + rows] for tap in range(3)
        ]
        mixed = jnp.dot(
            jnp.concatenate(windows, axis=1), weight[...], preferred_element_type=jnp.float32
        )
        out = layer_in_ref[offset + first : offset + first + rows].astype(jnp.float32) + mixed
        if follow:
            out = jnp.where(inside(edge_ref, first, rows), out, 0.0)
        out_ref[block] = out.astype(jnp.bfloat16)
        if follow:
            rel_ref[block] = jnp.dot(
                out_ref[block], turn_ref[...], preferred_element_type=jnp.float32
            ).astype(jnp.bfloat16)
            for part in parts(first, rows):
                activate(part, part, rel_ref, next_ref)


def layer(edges, pieces, active, layer_in, offset, length, spacing, turn=None):
    channels = active.shape[1]
    follow = turn is not None
    shape = (length, channels)
    outs = [(shape, jnp.bfloat16)]
    if follow:
        outs += [(shape, jnp.bfloat16)] * 2
    return call(
        lambda *refs: layer_kernel(*refs, spacing=spacing, offset=offset, follow=follow),
        "layer",
        [*pieces, active, layer_in] + ([turn] if follow else []),
        outs,
        [pltpu.VMEM((3 * channels, channels), jnp.bfloat16)],
        edges,
    )


def weight_kernel(active_ref, grad_ref, *outs, spacing, offset, halo, side):
    channels = active_ref.shape[1]
    length = grad_ref.shape[0] - 2 * halo
    half = channels // 2
    turned = active_ref[offset : offset + length, side * half : (side + 1) * half].T
    for tap in range(3):
        first = halo + (1 - tap) * spacing
        term = jnp.dot(
            turned, grad_ref[first : first + length], preferred_element_type=jnp.float32
        )
        if len(outs) == 3:
            outs[tap][...] = term.astype(jnp.bfloat16)
        else:
            outs[0][tap] = term


def weight_term(active, offset, grad_wide, side, spacing, halo):
    channels = active.shape[1]
    half = channels // 2
    if side == 0:
        outs = [((3, half, channels), jnp.float32)]
    else:
        outs = [((half, channels), jnp.bfloat16)] * 3
    out = call(
        lambda *refs: weight_kernel(*refs, spacing=spacing, offset=offset, halo=halo, side=side),
        "weight_term",
        [active, grad_wide],
        outs,
    )
    return out[0] if side == 0 else out


def pass_kernel(edge_ref, *refs, spacing, offset):
    pieces, refs = refs[:4], refs[4:]
    grad_ref, grad_rel_ref, layer_in_ref, turn_ref, out_ref, rel_ref, weight, act_grad = refs
    length, channels = out_ref.shape
    size = channels // 4
    for tap in range(3):
        for index, piece in enumerate(pieces):
            weight[index * size : (index + 1) * size, tap * channels : (tap + 1) * channels] = piece[tap]
    for first, rows in blocks_of(length):
        windows = [
            grad_ref[first + (2 - tap) * spacing : first + (2 - tap) * spacing + rows]
            for tap in range(3)
        ]
        act_grad[...] = lax.dot_general(
            jnp.concatenate(windows, axis=1),
            weight[...],
            (((1,), (1,)), ((), ())),
            preferred_element_type=jnp.float32,
        )
        for part in parts(first, rows):
            source = slice(offset + part.start, offset + part.stop)
            values = layer_in_ref[source].astype(jnp.float32)
            inv_rms = inverse_rms(values)
            normed = values * inv_rms
            slope = (
                cumulative_of(normed)
                + normed * jnp.exp(-0.5 * normed * normed) * 0.3989422804014327
            )
            norm_grad = act_grad[part.start - first : part.stop - first] * slope
            passed = grad_rel_ref[part].astype(jnp.float32) + inv_rms * (
                norm_grad - normed * jnp.mean(norm_grad * normed, axis=-1, keepdims=True)
            )
            passed = jnp.where(inside(edge_ref, part.start, CHUNK), passed, 0.0)
            rel_ref[part] = passed.astype(jnp.bfloat16)
        block = slice(first, first + rows)
        out_ref[block] = lax.dot_general(
            rel_ref[block], turn_ref[...], (((1,), (1,)), ((), ())), preferred_element_type=jnp.float32
        ).astype(jnp.bfloat16)


def pass_down(edges, pieces, grad_pad, grad_rel, layer_in, offset, turn, spacing):
    length = grad_pad.shape[0] - 2 * spacing
    channels = layer_in.shape[1]
    shape = (length, channels)
    return call(
        lambda *refs: pass_kernel(*refs, spacing=spacing, offset=offset),
        "pass_down",
        [*pieces, grad_pad, grad_rel, layer_in, turn],
        [(shape, jnp.bfloat16)],
        [
            pltpu.VMEM(shape, jnp.bfloat16),
            pltpu.VMEM((channels, 3 * channels), jnp.bfloat16),
            pltpu.VMEM((length // BLOCKS, channels), jnp.float32),
        ],
        edges,
    )[0]


def per_device(inputs, weight_one, weight_two, cotangent):
    count = lax.axis_size("seq")
    me = lax.axis_index("seq")
    length, channels = inputs.shape
    grad_scale = 1.0 / math.sqrt(length * count)
    block = weight_one.shape[0]
    routes = routes_of(count)
    turn_one = one_hot(count, routes[0], block)
    turn_two = one_hot(count, routes[1], block)

    back_rows = length + 2 * DILATION_A
    hidden_rows = length + 2 * DILATION_B

    def edges_of(rows, halo):
        first = jnp.where(me > 0, 0, halo)
        last = jnp.where(me < count - 1, rows, rows - halo)
        return jnp.stack([first, last]).astype(jnp.int32)

    odd = (me & 1) == 1
    scalars = lax.optimization_barrier(
        (
            edges_of(hidden_rows, DILATION_B),
            edges_of(back_rows, DILATION_A),
            edges_of(length, 0),
            odd.astype(jnp.int32).reshape(1),
            turn_one,
            turn_two,
        )
    )
    hidden_edges, back_edges, own_edges, odd_flag, turn_one, turn_two = scalars

    one, two = Gather(weight_one, routes[0]), Gather(weight_two, routes[1])

    def gather_both(*others):
        joined = two.join(*others)
        joined = one.join(joined)
        one.send()
        two.send()
        return joined

    one.send()
    edges_low = jnp.concatenate([inputs[:HALO], cotangent[:HALO]])
    edges_high = jnp.concatenate([inputs[length - HALO :], cotangent[length - HALO :]])
    inner = jnp.where(odd, edges_low, edges_high)
    outer = jnp.where(odd, edges_high, edges_low)
    joined = one.join(inner, outer, *scalars)
    one.send()
    two.held = after(two.held, joined)
    two.send()
    joined = one.join()
    one.send()
    joined = two.join(joined)
    two.send()
    for _ in range(one.steps - 3):
        joined = gather_both()
    across = [(i, i + 1) for i in range(1, count - 1, 2)] + [(i + 1, i) for i in range(1, count - 1, 2)]
    inner = lax.ppermute(after(inner, joined), "seq", core_pairs(count))
    outer = lax.ppermute(after(outer, joined), "seq", across)
    wide_in, wide_cot, active_one, cot_rel = first_active(
        odd_flag, inputs, cotangent, inner, outer, turn_one, turn_two, DILATION_B, back_rows
    )
    joined = gather_both(cot_rel)
    full_one = one.full()

    hidden, rel_two, active_two = layer(
        hidden_edges,
        full_one,
        after(active_one, joined),
        wide_in,
        DILATION_A,
        hidden_rows,
        DILATION_A,
        turn_two,
    )
    send_two = weight_term(active_two, DILATION_B, wide_cot, 1, DILATION_B, HALO)
    scatter_two = Scatter(send_two, routes[1])
    joined = two.join(*send_two)
    two.send()
    full_two = two.full()
    scatter_two.keep(
        weight_term(active_two, DILATION_B, after(wide_cot, joined), 0, DILATION_B, HALO)
    )
    sent = scatter_two.add()

    wide_grad = pass_down(
        back_edges,
        full_two,
        after(wide_cot, sent),
        cot_rel,
        rel_two,
        DILATION_B - DILATION_A,
        turn_two,
        DILATION_B,
    )

    send_one = weight_term(active_one, HALO, wide_grad, 1, DILATION_A, DILATION_A)
    scatter_one = Scatter(send_one, routes[0])
    keep_one = weight_term(active_one, HALO, after(wide_grad, *send_one), 0, DILATION_A, DILATION_A)
    scatter_one.keep(keep_one)
    sent = scatter_two.add(keep_one)
    sent = scatter_one.add(sent)
    own_rel = permute_channels(after(wide_grad, sent)[DILATION_A : DILATION_A + length], turn_one, 0)
    input_grad = pass_down(
        own_edges,
        full_one,
        wide_grad,
        own_rel,
        permute_channels(after(inputs, sent), turn_one, 0),
        0,
        turn_one,
        DILATION_A,
    )
    sent = scatter_two.add(input_grad)
    sent = scatter_one.add(sent)
    (outputs,) = layer(
        own_edges,
        full_two,
        after(active_two, sent),
        hidden,
        DILATION_B,
        length,
        DILATION_B,
    )
    rest = [outputs]
    while scatter_one.left:
        if scatter_two.left:
            rest = [scatter_two.add(*rest)]
        rest = [scatter_one.add(*rest)]
    grad_one = scatter_one.finish(grad_scale)
    grad_two = scatter_two.finish(grad_scale)
    return (outputs, input_grad, grad_one, grad_two)


def solution(mesh):
    in_specs = (P("seq", None), P("seq", None, None), P("seq", None, None), P("seq", None))
    out_specs = (P("seq", None), P("seq", None), P("seq", None, None), P("seq", None, None))
    return jax.shard_map(
        per_device, mesh=mesh, in_specs=in_specs, out_specs=out_specs, check_vma=False
    )
```

```python
import math

import jax
import jax.numpy as jnp
from jax import lax
from jax.experimental import pallas as pl
from jax.experimental.pallas import tpu as pltpu
from jax.sharding import PartitionSpec as P

DILATION_A = 32
DILATION_B = 64
HALO = DILATION_A + DILATION_B


def routes_of(count):
    bits = [1 << k for k in range(count.bit_length() - 2, 0, -1)]
    if len(bits) < 4:
        return [(bits, bits), (bits, bits)]
    far, (depth, row, column) = bits[:-3], bits[-3:]
    first = (far + [depth, column, row], far + [depth, row, column])
    second = (far + [column, depth, row], far + [row, depth, column])
    return [first, second]


def step_pairs(count, route, step):
    return [(i, i ^ route[i & 1][step]) for i in range(count)]


def core_pairs(count):
    return [(i, i ^ 1) for i in range(count)]


def relative_channels(count, route, block):
    position = jnp.arange(count * block)
    me = lax.axis_index("seq")
    index, offset = position // block, position % block
    half = count // 2
    other = index // half
    inner = index % half
    core = (me & 1) ^ other
    source = me ^ other
    for step in range(len(route[0])):
        bit = jnp.where(core == 0, route[0][step], route[1][step])
        source = source ^ jnp.where((inner >> step) & 1 == 1, bit, 0)
    return source * block + offset


def one_hot(count, route, block):
    channels = relative_channels(count, route, block)
    rows = lax.broadcasted_iota(jnp.int32, (count * block, count * block), 0)
    return (rows == channels[None, :]).astype(jnp.bfloat16)


def after(value, *others):
    return lax.optimization_barrier((value,) + others)[0]


class Gather:
    def __init__(self, shard, route):
        self.held = jnp.transpose(shard, (1, 0, 2))
        self.route = route
        self.steps = len(route[0])
        self.step = 0
        self.pieces = []

    def send(self):
        count = lax.axis_size("seq")
        if self.step < self.steps:
            self.arrived = lax.ppermute(self.held, "seq", step_pairs(count, self.route, self.step))
        if self.step >= self.steps - 1:
            self.pieces.append((self.held, lax.ppermute(self.held, "seq", core_pairs(count))))
        self.step += 1

    def join(self, *others):
        arrived = after(self.arrived, *others)
        if self.step < self.steps:
            arrived = join_rows(self.held, arrived)
        self.held = lax.optimization_barrier(arrived)
        return self.held

    def full(self):
        own, other = zip(*self.pieces)
        return own + other


class Scatter:
    def __init__(self, sends, route):
        self.route = route
        self.left = list(reversed(range(len(route[0]))))
        pairs = core_pairs(lax.axis_size("seq"))
        self.arrived = [lax.ppermute(send, "seq", pairs) for send in sends]

    def keep(self, keep):
        self.kept = keep

    def add(self, *others):
        arrived = self.arrived
        if isinstance(arrived, list):
            arrived = jnp.stack(lax.optimization_barrier(tuple(arrived) + others)[:3])
        else:
            arrived = after(arrived, *others)
        half = self.kept.shape[1] // 2
        send = (self.kept[:, half:] + arrived[:, half:].astype(jnp.float32)).astype(jnp.bfloat16)
        keep = self.kept[:, :half] + arrived[:, :half].astype(jnp.float32)
        send, self.kept = lax.optimization_barrier((send, keep))
        pairs = step_pairs(lax.axis_size("seq"), self.route, self.left.pop(0))
        self.arrived = lax.ppermute(send, "seq", pairs)
        return send

    def finish(self, grad_scale):
        return jnp.transpose((self.kept + self.arrived.astype(jnp.float32)) * grad_scale, (1, 0, 2))


def permute_channels(values, matrix, dim):
    return lax.dot_general(
        values, matrix, (((1,), (dim,)), ((), ())), preferred_element_type=jnp.float32
    ).astype(jnp.bfloat16)


CHUNK = 16
BLOCKS = 4
FREE = pl.CostEstimate(flops=0, bytes_accessed=0, transcendentals=0)


def on_chip(*arrays):
    return [pltpu.with_memory_space_constraint(array, pltpu.VMEM) for array in arrays]


def call(kernel, name, arrays, outs, scratch=(), edges=None, room=8):
    scalars = [] if edges is None else [edges]
    return pl.pallas_call(
        kernel,
        in_specs=[pl.BlockSpec(memory_space=pltpu.SMEM)] * len(scalars)
        + [pl.BlockSpec(memory_space=pltpu.VMEM)] * len(arrays),
        out_specs=[pl.BlockSpec(memory_space=pltpu.VMEM)] * len(outs),
        out_shape=[pltpu.VMEM(shape, dtype) for shape, dtype in outs],
        scratch_shapes=list(scratch),
        compiler_params=pltpu.CompilerParams(vmem_limit_bytes=room * 2**20),
        cost_estimate=FREE,
        name=name,
    )(*scalars, *on_chip(*arrays))


def over_blocks(length, body, unrolled):
    rows = length // BLOCKS

    def step(index, carry):
        body(index * rows, rows)
        return carry

    if unrolled:
        for index in range(BLOCKS):
            body(index * rows, rows)
    else:
        lax.fori_loop(0, BLOCKS, step, 0)


def span(first, rows):
    return pl.ds(first if isinstance(first, int) else pl.multiple_of(first, CHUNK), rows)


def inverse_rms(values):
    return lax.rsqrt(jnp.mean(values * values, axis=-1, keepdims=True) + 1e-06)


def cumulative_of(normed):
    return 0.5 * (1.0 + lax.erf(normed * 0.7071067811865476))


def activate(first, rel_ref, active_ref):
    for start in range(0, rel_ref.shape[0], CHUNK):
        values = rel_ref[start : start + CHUNK].astype(jnp.float32)
        normed = values * inverse_rms(values)
        active_ref[span(first + start, CHUNK)] = (normed * cumulative_of(normed)).astype(jnp.bfloat16)


def inside(edge_ref, first, rows):
    row = first + lax.broadcasted_iota(jnp.int32, (rows, 1), 0)
    return (row >= edge_ref[0]) & (row < edge_ref[1])


def join_kernel(first_ref, second_ref, out_ref):
    rows = first_ref.shape[1]
    out_ref[:, :rows] = first_ref[...]
    out_ref[:, rows:] = second_ref[...]


def join_rows(first, second):
    taps, rows, channels = first.shape
    if rows % 16:
        return jnp.concatenate([first, second], axis=1)
    shape = (taps, 2 * rows, channels)
    return call(join_kernel, "join_rows", [first, second], [(shape, first.dtype)], room=4)[0]


def active_kernel(
    odd_ref, layer_in_ref, grad_ref, inner_ref, outer_ref, turn_ref, next_turn_ref,
    wide_in_ref, wide_grad_ref, active_ref, grad_rel_ref, rel_ref, *, offset
):
    length = layer_in_ref.shape[0]
    halo = inner_ref.shape[0] // 2
    odd = odd_ref[0] == 1
    for index, (wide_ref, own_ref) in enumerate(((wide_in_ref, layer_in_ref), (wide_grad_ref, grad_ref))):
        rows = slice(index * halo, (index + 1) * halo)
        wide_ref[:halo] = jnp.where(odd, inner_ref[rows], outer_ref[rows])
        wide_ref[halo : halo + length] = own_ref[...]
        wide_ref[halo + length :] = jnp.where(odd, outer_ref[rows], inner_ref[rows])

    def own_block(first, rows):
        rel_ref[...] = jnp.dot(
            wide_in_ref[span(first, rows)], turn_ref[...], preferred_element_type=jnp.float32
        ).astype(jnp.bfloat16)
        activate(first, rel_ref, active_ref)

    def grad_block(first, rows):
        grad_rel_ref[span(first, rows)] = jnp.dot(
            wide_grad_ref[span(offset + first, rows)],
            next_turn_ref[...],
            preferred_element_type=jnp.float32,
        ).astype(jnp.bfloat16)

    over_blocks(wide_in_ref.shape[0], own_block, False)
    over_blocks(grad_rel_ref.shape[0], grad_block, False)


def first_active(odd, layer_in, grad, inner, outer, turn, next_turn, offset, back_rows):
    length, channels = layer_in.shape
    rows = length + inner.shape[0]
    wide = ((rows, channels), jnp.bfloat16)
    return call(
        lambda *refs: active_kernel(*refs, offset=offset),
        "first_active",
        [layer_in, grad, inner, outer, turn, next_turn],
        [wide, wide, wide, ((back_rows, channels), jnp.bfloat16)],
        [pltpu.VMEM((rows // BLOCKS, channels), jnp.bfloat16)],
        odd,
        room=6,
    )


def layer_kernel(edge_ref, *refs, spacing, offset, follow):
    pieces, (active_ref, layer_in_ref, *refs) = refs[:4], refs[4:]
    if follow:
        turn_ref, out_ref, rel_ref, next_ref, weight = refs
    else:
        out_ref, weight = refs
    length, channels = out_ref.shape
    size = channels // 4
    for tap in range(3):
        for index, piece in enumerate(pieces):
            first = tap * channels + index * size
            weight[first : first + size] = piece[tap]

    def block(first, rows):
        windows = [active_ref[span(first + tap * spacing, rows)] for tap in range(3)]
        mixed = jnp.dot(
            jnp.concatenate(windows, axis=1), weight[...], preferred_element_type=jnp.float32
        )
        out = layer_in_ref[span(offset + first, rows)].astype(jnp.float32) + mixed
        if follow:
            out = jnp.where(inside(edge_ref, first, rows), out, 0.0)
        out = out.astype(jnp.bfloat16)
        out_ref[span(first, rows)] = out
        if follow:
            rel_ref[span(first, rows)] = jnp.dot(
                out, turn_ref[...], preferred_element_type=jnp.float32
            ).astype(jnp.bfloat16)
            activate(first, rel_ref.at[span(first, rows)], next_ref)

    over_blocks(length, block, follow)


def layer(edges, pieces, active, layer_in, offset, length, spacing, turn=None):
    channels = active.shape[1]
    follow = turn is not None
    shape = (length, channels)
    outs = [(shape, jnp.bfloat16)]
    if follow:
        outs += [(shape, jnp.bfloat16)] * 2
    return call(
        lambda *refs: layer_kernel(*refs, spacing=spacing, offset=offset, follow=follow),
        "layer",
        [*pieces, active, layer_in] + ([turn] if follow else []),
        outs,
        [pltpu.VMEM((3 * channels, channels), jnp.bfloat16)],
        edges,
    )


def weight_kernel(active_ref, grad_ref, *outs, spacing, offset, halo, side):
    channels = active_ref.shape[1]
    length = grad_ref.shape[0] - 2 * halo
    half = channels // 2
    turned = active_ref[offset : offset + length, side * half : (side + 1) * half].T
    for tap in range(3):
        first = halo + (1 - tap) * spacing
        term = jnp.dot(
            turned, grad_ref[first : first + length], preferred_element_type=jnp.float32
        )
        if len(outs) == 3:
            outs[tap][...] = term.astype(jnp.bfloat16)
        else:
            outs[0][tap] = term


def weight_term(active, offset, grad_wide, side, spacing, halo):
    channels = active.shape[1]
    half = channels // 2
    if side == 0:
        outs = [((3, half, channels), jnp.float32)]
    else:
        outs = [((half, channels), jnp.bfloat16)] * 3
    out = call(
        lambda *refs: weight_kernel(*refs, spacing=spacing, offset=offset, halo=halo, side=side),
        "weight_term",
        [active, grad_wide],
        outs,
    )
    return out[0] if side == 0 else out


def pass_kernel(edge_ref, *refs, spacing, offset, unrolled):
    pieces, refs = refs[:4], refs[4:]
    grad_ref, grad_rel_ref, layer_in_ref, turn_ref, out_ref, rel_ref, weight, act_grad = refs
    length, channels = out_ref.shape
    size = channels // 4
    for tap in range(3):
        for index, piece in enumerate(pieces):
            weight[index * size : (index + 1) * size, tap * channels : (tap + 1) * channels] = piece[tap]

    def block(first, rows):
        windows = [grad_ref[span(first + (2 - tap) * spacing, rows)] for tap in range(3)]
        act_grad[...] = lax.dot_general(
            jnp.concatenate(windows, axis=1),
            weight[...],
            (((1,), (1,)), ((), ())),
            preferred_element_type=jnp.float32,
        )
        for start in range(0, rows, CHUNK):
            values = layer_in_ref[span(offset + first + start, CHUNK)].astype(jnp.float32)
            inv_rms = inverse_rms(values)
            normed = values * inv_rms
            slope = (
                cumulative_of(normed)
                + normed * jnp.exp(-0.5 * normed * normed) * 0.3989422804014327
            )
            norm_grad = act_grad[start : start + CHUNK] * slope
            passed = grad_rel_ref[span(first + start, CHUNK)].astype(jnp.float32) + inv_rms * (
                norm_grad - normed * jnp.mean(norm_grad * normed, axis=-1, keepdims=True)
            )
            passed = jnp.where(inside(edge_ref, first + start, CHUNK), passed, 0.0)
            rel_ref[start : start + CHUNK] = passed.astype(jnp.bfloat16)
        out_ref[span(first, rows)] = lax.dot_general(
            rel_ref[...], turn_ref[...], (((1,), (1,)), ((), ())), preferred_element_type=jnp.float32
        ).astype(jnp.bfloat16)

    over_blocks(length, block, unrolled)


def pass_down(edges, pieces, grad_pad, grad_rel, layer_in, offset, turn, spacing, unrolled):
    length = grad_pad.shape[0] - 2 * spacing
    channels = layer_in.shape[1]
    shape = (length, channels)
    return call(
        lambda *refs: pass_kernel(*refs, spacing=spacing, offset=offset, unrolled=unrolled),
        "pass_down",
        [*pieces, grad_pad, grad_rel, layer_in, turn],
        [(shape, jnp.bfloat16)],
        [
            pltpu.VMEM((length // BLOCKS, channels), jnp.bfloat16),
            pltpu.VMEM((channels, 3 * channels), jnp.bfloat16),
            pltpu.VMEM((length // BLOCKS, channels), jnp.float32),
        ],
        edges,
    )[0]


def per_device(inputs, weight_one, weight_two, cotangent):
    count = lax.axis_size("seq")
    me = lax.axis_index("seq")
    length, channels = inputs.shape
    grad_scale = 1.0 / math.sqrt(length * count)
    block = weight_one.shape[0]
    routes = routes_of(count)
    turn_one = one_hot(count, routes[0], block)
    turn_two = one_hot(count, routes[1], block)

    back_rows = length + 2 * DILATION_A
    hidden_rows = length + 2 * DILATION_B

    def edges_of(rows, halo):
        first = jnp.where(me > 0, 0, halo)
        last = jnp.where(me < count - 1, rows, rows - halo)
        return jnp.stack([first, last]).astype(jnp.int32)

    odd = (me & 1) == 1
    scalars = lax.optimization_barrier(
        (
            edges_of(hidden_rows, DILATION_B),
            edges_of(back_rows, DILATION_A),
            edges_of(length, 0),
            odd.astype(jnp.int32).reshape(1),
            turn_one,
            turn_two,
        )
    )
    hidden_edges, back_edges, own_edges, odd_flag, turn_one, turn_two = scalars

    one, two = Gather(weight_one, routes[0]), Gather(weight_two, routes[1])

    def gather_both(*others):
        joined = two.join(*others)
        joined = one.join(joined)
        one.send()
        two.send()
        return joined

    one.send()
    edges_low = jnp.concatenate([inputs[:HALO], cotangent[:HALO]])
    edges_high = jnp.concatenate([inputs[length - HALO :], cotangent[length - HALO :]])
    inner = jnp.where(odd, edges_low, edges_high)
    outer = jnp.where(odd, edges_high, edges_low)
    joined = one.join(inner, outer, *scalars)
    one.send()
    two.held = after(two.held, joined)
    two.send()
    across = [(i, i + 1) for i in range(1, count - 1, 2)] + [(i + 1, i) for i in range(1, count - 1, 2)]
    inner = lax.ppermute(after(inner, joined), "seq", core_pairs(count))
    outer = lax.ppermute(after(outer, joined), "seq", across)
    joined = one.join()
    one.send()
    joined = two.join(joined, inner, outer)
    two.send()
    for _ in range(one.steps - 3):
        joined = gather_both()
    wide_in, wide_cot, active_one, cot_rel = first_active(
        odd_flag, inputs, cotangent, inner, outer, turn_one, turn_two, DILATION_B, back_rows
    )
    joined = gather_both(cot_rel)
    full_one = one.full()

    hidden, rel_two, active_two = layer(
        hidden_edges,
        full_one,
        after(active_one, joined),
        wide_in,
        DILATION_A,
        hidden_rows,
        DILATION_A,
        turn_two,
    )
    send_two = weight_term(active_two, DILATION_B, wide_cot, 1, DILATION_B, HALO)
    scatter_two = Scatter(send_two, routes[1])
    joined = two.join(*send_two)
    two.send()
    full_two = two.full()
    scatter_two.keep(
        weight_term(active_two, DILATION_B, after(wide_cot, joined), 0, DILATION_B, HALO)
    )
    sent = scatter_two.add()

    wide_grad = pass_down(
        back_edges,
        full_two,
        after(wide_cot, sent),
        cot_rel,
        rel_two,
        DILATION_B - DILATION_A,
        turn_two,
        DILATION_B,
        True,
    )

    send_one = weight_term(active_one, HALO, wide_grad, 1, DILATION_A, DILATION_A)
    scatter_one = Scatter(send_one, routes[0])
    keep_one = weight_term(active_one, HALO, after(wide_grad, *send_one), 0, DILATION_A, DILATION_A)
    scatter_one.keep(keep_one)
    sent = scatter_two.add(keep_one)
    sent = scatter_one.add(sent)
    own_rel = permute_channels(after(wide_grad, sent)[DILATION_A : DILATION_A + length], turn_one, 0)
    input_grad = pass_down(
        own_edges,
        full_one,
        wide_grad,
        own_rel,
        permute_channels(after(inputs, sent), turn_one, 0),
        0,
        turn_one,
        DILATION_A,
        False,
    )
    sent = scatter_two.add(input_grad)
    sent = scatter_one.add(sent)
    (outputs,) = layer(
        own_edges,
        full_two,
        after(active_two, sent),
        hidden,
        DILATION_B,
        length,
        DILATION_B,
    )
    rest = [outputs]
    while scatter_one.left:
        if scatter_two.left:
            rest = [scatter_two.add(*rest)]
        rest = [scatter_one.add(*rest)]
    grad_one = scatter_one.finish(grad_scale)
    grad_two = scatter_two.finish(grad_scale)
    return (outputs, input_grad, grad_one, grad_two)


def solution(mesh):
    in_specs = (P("seq", None), P("seq", None, None), P("seq", None, None), P("seq", None))
    out_specs = (P("seq", None), P("seq", None), P("seq", None, None), P("seq", None, None))
    return jax.shard_map(
        per_device, mesh=mesh, in_specs=in_specs, out_specs=out_specs, check_vma=False
    )
```

```python
import math

import jax
import jax.numpy as jnp
from jax import lax
from jax.experimental import pallas as pl
from jax.experimental.pallas import tpu as pltpu
from jax.sharding import PartitionSpec as P

DILATION_A = 32
DILATION_B = 64
HALO = DILATION_A + DILATION_B


def routes_of(count):
    bits = [1 << k for k in range(count.bit_length() - 2, 0, -1)]
    if len(bits) < 4:
        return [(bits, bits), (bits, bits)]
    far, (depth, row, column) = bits[:-3], bits[-3:]
    first = (far + [depth, column, row], far + [depth, row, column])
    second = (far + [column, depth, row], far + [row, depth, column])
    return [first, second]


def step_pairs(count, route, step):
    return [(i, i ^ route[i & 1][step]) for i in range(count)]


def core_pairs(count):
    return [(i, i ^ 1) for i in range(count)]


def relative_channels(count, route, block):
    position = jnp.arange(count * block)
    me = lax.axis_index("seq")
    index, offset = position // block, position % block
    half = count // 2
    other = index // half
    inner = index % half
    core = (me & 1) ^ other
    source = me ^ other
    for step in range(len(route[0])):
        bit = jnp.where(core == 0, route[0][step], route[1][step])
        source = source ^ jnp.where((inner >> step) & 1 == 1, bit, 0)
    return source * block + offset


def one_hot(count, route, block):
    channels = relative_channels(count, route, block)
    rows = lax.broadcasted_iota(jnp.int32, (count * block, count * block), 0)
    return (rows == channels[None, :]).astype(jnp.bfloat16)


def after(value, *others):
    return lax.optimization_barrier((value,) + others)[0]


class Gather:
    def __init__(self, shard, route):
        self.held = jnp.transpose(shard, (1, 0, 2))
        self.route = route
        self.steps = len(route[0])
        self.step = 0
        self.pieces = []

    def send(self):
        count = lax.axis_size("seq")
        if self.step < self.steps:
            self.arrived = lax.ppermute(self.held, "seq", step_pairs(count, self.route, self.step))
        if self.step >= self.steps - 1:
            self.pieces.append((self.held, lax.ppermute(self.held, "seq", core_pairs(count))))
        self.step += 1

    def join(self, *others):
        arrived = after(self.arrived, *others)
        if self.step < self.steps:
            arrived = join_rows(self.held, arrived)
        self.held = lax.optimization_barrier(arrived)
        return self.held

    def full(self):
        own, other = zip(*self.pieces)
        return own + other


class Scatter:
    def __init__(self, sends, route):
        self.route = route
        self.left = list(reversed(range(len(route[0]))))
        pairs = core_pairs(lax.axis_size("seq"))
        self.arrived = [lax.ppermute(send, "seq", pairs) for send in sends]

    def keep(self, keep):
        self.kept = keep

    def add(self, *others):
        return self.go(self.total(*others))

    def total(self, *others):
        arrived = self.arrived
        if isinstance(arrived, list):
            arrived = jnp.stack(lax.optimization_barrier(tuple(arrived) + others)[:3])
        else:
            arrived = after(arrived, *others)
        half = self.kept.shape[1] // 2
        send = (self.kept[:, half:] + arrived[:, half:].astype(jnp.float32)).astype(jnp.bfloat16)
        keep = self.kept[:, :half] + arrived[:, :half].astype(jnp.float32)
        send, self.kept = lax.optimization_barrier((send, keep))
        return send

    def go(self, send, *others):
        if others:
            send = after(send, *others)
        pairs = step_pairs(lax.axis_size("seq"), self.route, self.left.pop(0))
        self.arrived = lax.ppermute(send, "seq", pairs)
        return send

    def finish(self, grad_scale):
        return jnp.transpose((self.kept + self.arrived.astype(jnp.float32)) * grad_scale, (1, 0, 2))


CHUNK = 16
BLOCKS = 4
FREE = pl.CostEstimate(flops=0, bytes_accessed=0, transcendentals=0)


def on_chip(*arrays):
    return [pltpu.with_memory_space_constraint(array, pltpu.VMEM) for array in arrays]


def call(kernel, name, arrays, outs, scratch=(), edges=None, room=8):
    scalars = [] if edges is None else [edges]
    return pl.pallas_call(
        kernel,
        in_specs=[pl.BlockSpec(memory_space=pltpu.SMEM)] * len(scalars)
        + [pl.BlockSpec(memory_space=pltpu.VMEM)] * len(arrays),
        out_specs=[pl.BlockSpec(memory_space=pltpu.VMEM)] * len(outs),
        out_shape=[pltpu.VMEM(shape, dtype) for shape, dtype in outs],
        scratch_shapes=list(scratch),
        compiler_params=pltpu.CompilerParams(vmem_limit_bytes=room * 2**20),
        cost_estimate=FREE,
        name=name,
    )(*scalars, *on_chip(*arrays))


def over_blocks(length, body, unrolled):
    rows = length // BLOCKS

    def step(index, carry):
        body(index * rows, rows)
        return carry

    if unrolled:
        for index in range(BLOCKS):
            body(index * rows, rows)
    else:
        lax.fori_loop(0, BLOCKS, step, 0)


def span(first, rows):
    return pl.ds(first if isinstance(first, int) else pl.multiple_of(first, CHUNK), rows)


def inverse_rms(values):
    return lax.rsqrt(jnp.mean(values * values, axis=-1, keepdims=True) + 1e-06)


def cumulative_of(normed):
    return 0.5 * (1.0 + lax.erf(normed * 0.7071067811865476))


def activate(first, rel_ref, active_ref):
    for start in range(0, rel_ref.shape[0], CHUNK):
        values = rel_ref[start : start + CHUNK].astype(jnp.float32)
        normed = values * inverse_rms(values)
        active_ref[span(first + start, CHUNK)] = (normed * cumulative_of(normed)).astype(jnp.bfloat16)


def inside(edge_ref, first, rows):
    row = first + lax.broadcasted_iota(jnp.int32, (rows, 1), 0)
    return (row >= edge_ref[0]) & (row < edge_ref[1])


def join_kernel(first_ref, second_ref, out_ref):
    rows = first_ref.shape[1]
    out_ref[:, :rows] = first_ref[...]
    out_ref[:, rows:] = second_ref[...]


def join_rows(first, second):
    taps, rows, channels = first.shape
    if rows % 16:
        return jnp.concatenate([first, second], axis=1)
    shape = (taps, 2 * rows, channels)
    return call(join_kernel, "join_rows", [first, second], [(shape, first.dtype)], room=4)[0]


def active_kernel(
    odd_ref, layer_in_ref, grad_ref, inner_ref, outer_ref, turn_ref, next_turn_ref,
    wide_in_ref, wide_grad_ref, active_ref, rel_ref, grad_rel_ref, *, offset
):
    length = layer_in_ref.shape[0]
    halo = inner_ref.shape[0] // 2
    odd = odd_ref[0] == 1
    for index, (wide_ref, own_ref) in enumerate(((wide_in_ref, layer_in_ref), (wide_grad_ref, grad_ref))):
        rows = slice(index * halo, (index + 1) * halo)
        wide_ref[:halo] = jnp.where(odd, inner_ref[rows], outer_ref[rows])
        wide_ref[halo : halo + length] = own_ref[...]
        wide_ref[halo + length :] = jnp.where(odd, outer_ref[rows], inner_ref[rows])

    def own_block(first, rows):
        rel_ref[span(first, rows)] = jnp.dot(
            wide_in_ref[span(first, rows)], turn_ref[...], preferred_element_type=jnp.float32
        ).astype(jnp.bfloat16)
        activate(first, rel_ref.at[span(first, rows)], active_ref)

    def grad_block(first, rows):
        grad_rel_ref[span(first, rows)] = jnp.dot(
            wide_grad_ref[span(offset + first, rows)],
            next_turn_ref[...],
            preferred_element_type=jnp.float32,
        ).astype(jnp.bfloat16)

    over_blocks(wide_in_ref.shape[0], own_block, False)
    over_blocks(grad_rel_ref.shape[0], grad_block, False)


def first_active(odd, layer_in, grad, inner, outer, turn, next_turn, offset, back_rows):
    length, channels = layer_in.shape
    rows = length + inner.shape[0]
    wide = ((rows, channels), jnp.bfloat16)
    return call(
        lambda *refs: active_kernel(*refs, offset=offset),
        "first_active",
        [layer_in, grad, inner, outer, turn, next_turn],
        [wide, wide, wide, wide, ((back_rows, channels), jnp.bfloat16)],
        (),
        odd,
        room=6,
    )


def layer_kernel(edge_ref, *refs, spacing, offset, follow):
    pieces, (active_ref, layer_in_ref, *refs) = refs[:4], refs[4:]
    if follow:
        turn_ref, out_ref, rel_ref, next_ref, weight = refs
    else:
        out_ref, weight = refs
    length, channels = out_ref.shape
    size = channels // 4
    for tap in range(3):
        for index, piece in enumerate(pieces):
            first = tap * channels + index * size
            weight[first : first + size] = piece[tap]

    def block(first, rows):
        windows = [active_ref[span(first + tap * spacing, rows)] for tap in range(3)]
        mixed = jnp.dot(
            jnp.concatenate(windows, axis=1), weight[...], preferred_element_type=jnp.float32
        )
        out = layer_in_ref[span(offset + first, rows)].astype(jnp.float32) + mixed
        if follow:
            out = jnp.where(inside(edge_ref, first, rows), out, 0.0)
        out = out.astype(jnp.bfloat16)
        out_ref[span(first, rows)] = out
        if follow:
            rel_ref[span(first, rows)] = jnp.dot(
                out, turn_ref[...], preferred_element_type=jnp.float32
            ).astype(jnp.bfloat16)
            activate(first, rel_ref.at[span(first, rows)], next_ref)

    over_blocks(length, block, follow)


def layer(edges, pieces, active, layer_in, offset, length, spacing, turn=None):
    channels = active.shape[1]
    follow = turn is not None
    shape = (length, channels)
    outs = [(shape, jnp.bfloat16)]
    if follow:
        outs += [(shape, jnp.bfloat16)] * 2
    return call(
        lambda *refs: layer_kernel(*refs, spacing=spacing, offset=offset, follow=follow),
        "layer",
        [*pieces, active, layer_in] + ([turn] if follow else []),
        outs,
        [pltpu.VMEM((3 * channels, channels), jnp.bfloat16)],
        edges,
    )


def weight_kernel(active_ref, grad_ref, *outs, spacing, offset, halo, side):
    channels = active_ref.shape[1]
    length = grad_ref.shape[0] - 2 * halo
    half = channels // 2
    turned = active_ref[offset : offset + length, side * half : (side + 1) * half].T
    for tap in range(3):
        first = halo + (1 - tap) * spacing
        term = jnp.dot(
            turned, grad_ref[first : first + length], preferred_element_type=jnp.float32
        )
        if len(outs) == 3:
            outs[tap][...] = term.astype(jnp.bfloat16)
        else:
            outs[0][tap] = term


def weight_term(active, offset, grad_wide, side, spacing, halo):
    channels = active.shape[1]
    half = channels // 2
    if side == 0:
        outs = [((3, half, channels), jnp.float32)]
    else:
        outs = [((half, channels), jnp.bfloat16)] * 3
    out = call(
        lambda *refs: weight_kernel(*refs, spacing=spacing, offset=offset, halo=halo, side=side),
        "weight_term",
        [active, grad_wide],
        outs,
    )
    return out[0] if side == 0 else out


def pass_kernel(edge_ref, *refs, spacing, offset, unrolled):
    pieces, refs = refs[:4], refs[4:]
    grad_ref, layer_in_ref, turn_ref, *refs = refs
    grad_rel_ref, out_ref, rel_ref, weight, act_grad = refs if unrolled else refs[-1:] + refs[:-1]
    length, channels = out_ref.shape
    size = channels // 4
    for tap in range(3):
        for index, piece in enumerate(pieces):
            weight[index * size : (index + 1) * size, tap * channels : (tap + 1) * channels] = piece[tap]

    def block(first, rows):
        windows = [grad_ref[span(first + (2 - tap) * spacing, rows)] for tap in range(3)]
        act_grad[...] = lax.dot_general(
            jnp.concatenate(windows, axis=1),
            weight[...],
            (((1,), (1,)), ((), ())),
            preferred_element_type=jnp.float32,
        )
        if not unrolled:
            grad_rel_ref[...] = jnp.dot(
                grad_ref[span(first + spacing, rows)], turn_ref[...], preferred_element_type=jnp.float32
            ).astype(jnp.bfloat16)
        for start in range(0, rows, CHUNK):
            values = layer_in_ref[span(offset + first + start, CHUNK)].astype(jnp.float32)
            inv_rms = inverse_rms(values)
            normed = values * inv_rms
            slope = (
                cumulative_of(normed)
                + normed * jnp.exp(-0.5 * normed * normed) * 0.3989422804014327
            )
            norm_grad = act_grad[start : start + CHUNK] * slope
            passed = grad_rel_ref[span(first + start if unrolled else start, CHUNK)].astype(jnp.float32) + inv_rms * (
                norm_grad - normed * jnp.mean(norm_grad * normed, axis=-1, keepdims=True)
            )
            passed = jnp.where(inside(edge_ref, first + start, CHUNK), passed, 0.0)
            rel_ref[start : start + CHUNK] = passed.astype(jnp.bfloat16)
        out_ref[span(first, rows)] = lax.dot_general(
            rel_ref[...], turn_ref[...], (((1,), (1,)), ((), ())), preferred_element_type=jnp.float32
        ).astype(jnp.bfloat16)

    over_blocks(length, block, unrolled)


def pass_down(edges, pieces, grad_pad, layer_in, offset, turn, spacing, grad_rel=None):
    length = grad_pad.shape[0] - 2 * spacing
    channels = layer_in.shape[1]
    unrolled = grad_rel is not None
    shape = (length, channels)
    return call(
        lambda *refs: pass_kernel(*refs, spacing=spacing, offset=offset, unrolled=unrolled),
        "pass_down",
        [*pieces, grad_pad, layer_in, turn] + ([grad_rel] if unrolled else []),
        [(shape, jnp.bfloat16)],
        [
            pltpu.VMEM((length // BLOCKS, channels), jnp.bfloat16),
            pltpu.VMEM((channels, 3 * channels), jnp.bfloat16),
            pltpu.VMEM((length // BLOCKS, channels), jnp.float32),
        ]
        + [pltpu.VMEM((length // BLOCKS, channels), jnp.bfloat16)] * (not unrolled),
        edges,
    )[0]


def per_device(inputs, weight_one, weight_two, cotangent):
    count = lax.axis_size("seq")
    me = lax.axis_index("seq")
    length, channels = inputs.shape
    grad_scale = 1.0 / math.sqrt(length * count)
    block = weight_one.shape[0]
    routes = routes_of(count)
    turn_one = one_hot(count, routes[0], block)
    turn_two = one_hot(count, routes[1], block)

    back_rows = length + 2 * DILATION_A
    hidden_rows = length + 2 * DILATION_B

    def edges_of(rows, halo):
        first = jnp.where(me > 0, 0, halo)
        last = jnp.where(me < count - 1, rows, rows - halo)
        return jnp.stack([first, last]).astype(jnp.int32)

    odd = (me & 1) == 1
    scalars = lax.optimization_barrier(
        (
            edges_of(hidden_rows, DILATION_B),
            edges_of(back_rows, DILATION_A),
            edges_of(length, 0),
            odd.astype(jnp.int32).reshape(1),
            turn_one,
            turn_two,
        )
    )
    hidden_edges, back_edges, own_edges, odd_flag, turn_one, turn_two = scalars

    one, two = Gather(weight_one, routes[0]), Gather(weight_two, routes[1])

    def gather_both(*others):
        joined = two.join(*others)
        joined = one.join(joined)
        one.send()
        two.send()
        return joined

    one.send()
    edges_low = jnp.concatenate([inputs[:HALO], cotangent[:HALO]])
    edges_high = jnp.concatenate([inputs[length - HALO :], cotangent[length - HALO :]])
    inner = jnp.where(odd, edges_low, edges_high)
    outer = jnp.where(odd, edges_high, edges_low)
    joined = one.join(inner, outer, *scalars)
    one.send()
    two.held = after(two.held, joined)
    two.send()
    across = [(i, i + 1) for i in range(1, count - 1, 2)] + [(i + 1, i) for i in range(1, count - 1, 2)]
    inner = lax.ppermute(after(inner, joined), "seq", core_pairs(count))
    outer = lax.ppermute(after(outer, joined), "seq", across)
    joined = one.join()
    one.send()
    joined = two.join(joined, inner, outer)
    two.send()
    for _ in range(one.steps - 3):
        joined = gather_both()
    wide_in, wide_cot, active_one, rel_one, cot_rel = first_active(
        odd_flag, inputs, cotangent, inner, outer, turn_one, turn_two, DILATION_B, back_rows
    )
    joined = gather_both(cot_rel)
    full_one = one.full()

    hidden, rel_two, active_two = layer(
        hidden_edges,
        full_one,
        after(active_one, joined),
        wide_in,
        DILATION_A,
        hidden_rows,
        DILATION_A,
        turn_two,
    )
    send_two = weight_term(active_two, DILATION_B, wide_cot, 1, DILATION_B, HALO)
    scatter_two = Scatter(send_two, routes[1])
    joined = two.join(*send_two)
    two.send()
    full_two = two.full()
    scatter_two.keep(
        weight_term(active_two, DILATION_B, after(wide_cot, joined), 0, DILATION_B, HALO)
    )
    sent = scatter_two.add()

    wide_grad = pass_down(
        back_edges,
        full_two,
        after(wide_cot, sent),
        rel_two,
        DILATION_B - DILATION_A,
        turn_two,
        DILATION_B,
        cot_rel,
    )

    send_one = weight_term(active_one, HALO, wide_grad, 1, DILATION_A, DILATION_A)
    scatter_one = Scatter(send_one, routes[0])
    keep_one = weight_term(active_one, HALO, after(wide_grad, *send_one), 0, DILATION_A, DILATION_A)
    scatter_one.keep(keep_one)
    send = scatter_two.total(keep_one)
    sent = scatter_one.add(send)
    sent = scatter_two.go(send, sent)
    input_grad = pass_down(
        own_edges,
        full_one,
        after(wide_grad, sent),
        rel_one,
        HALO,
        turn_one,
        DILATION_A,
    )
    sent = scatter_two.add(input_grad)
    sent = scatter_one.add(sent)
    (outputs,) = layer(
        own_edges,
        full_two,
        after(active_two, sent),
        hidden,
        DILATION_B,
        length,
        DILATION_B,
    )
    rest = [outputs]
    while scatter_one.left:
        if scatter_two.left:
            rest = [scatter_two.add(*rest)]
        rest = [scatter_one.add(*rest)]
    grad_one = scatter_one.finish(grad_scale)
    grad_two = scatter_two.finish(grad_scale)
    return (outputs, input_grad, grad_one, grad_two)


def solution(mesh):
    in_specs = (P("seq", None), P("seq", None, None), P("seq", None, None), P("seq", None))
    out_specs = (P("seq", None), P("seq", None), P("seq", None, None), P("seq", None, None))
    return jax.shard_map(
        per_device, mesh=mesh, in_specs=in_specs, out_specs=out_specs, check_vma=False
    )
```

```python
import math

import jax
import jax.numpy as jnp
from jax import lax
from jax.experimental import pallas as pl
from jax.experimental.pallas import tpu as pltpu
from jax.sharding import PartitionSpec as P

DILATION_A = 32
DILATION_B = 64
HALO = DILATION_A + DILATION_B


def routes_of(count):
    bits = [1 << k for k in range(count.bit_length() - 2, 0, -1)]
    if len(bits) < 4:
        return [(bits, bits), (bits, bits)]
    far, (depth, row, column) = bits[:-3], bits[-3:]
    first = (far + [depth, column, row], far + [depth, row, column])
    second = (far + [column, depth, row], far + [row, depth, column])
    return [first, second]


def step_pairs(count, route, step):
    return [(i, i ^ route[i & 1][step]) for i in range(count)]


def core_pairs(count):
    return [(i, i ^ 1) for i in range(count)]


def relative_channels(count, route, block):
    position = jnp.arange(count * block)
    me = lax.axis_index("seq")
    index, offset = position // block, position % block
    half = count // 2
    other = index // half
    inner = index % half
    core = (me & 1) ^ other
    source = me ^ other
    for step in range(len(route[0])):
        bit = jnp.where(core == 0, route[0][step], route[1][step])
        source = source ^ jnp.where((inner >> step) & 1 == 1, bit, 0)
    return source * block + offset


def one_hot(count, route, block):
    channels = relative_channels(count, route, block)
    rows = lax.broadcasted_iota(jnp.int32, (count * block, count * block), 0)
    return (rows == channels[None, :]).astype(jnp.bfloat16)


def after(value, *others):
    return lax.optimization_barrier((value,) + others)[0]


class Gather:
    def __init__(self, shard, route):
        self.held = jnp.transpose(shard, (1, 0, 2))
        self.route = route
        self.steps = len(route[0])
        self.step = 0
        self.pieces = []

    def send(self):
        count = lax.axis_size("seq")
        if self.step < self.steps:
            self.arrived = lax.ppermute(self.held, "seq", step_pairs(count, self.route, self.step))
        if self.step >= self.steps - 1:
            self.pieces.append((self.held, lax.ppermute(self.held, "seq", core_pairs(count))))
        self.step += 1

    def join(self, *others):
        arrived = after(self.arrived, *others)
        if self.step < self.steps:
            arrived = join_rows(self.held, arrived)
        self.held = lax.optimization_barrier(arrived)
        return self.held

    def full(self):
        own, other = zip(*self.pieces)
        return own + other


class Scatter:
    def __init__(self, sends, route):
        self.route = route
        self.left = list(reversed(range(len(route[0]))))
        pairs = core_pairs(lax.axis_size("seq"))
        self.arrived = [lax.ppermute(send, "seq", pairs) for send in sends]

    def keep(self, keep):
        self.kept = keep

    def add(self, *others):
        return self.go(self.total(*others))

    def total(self, *others):
        arrived = self.arrived
        if isinstance(arrived, list):
            arrived = jnp.stack(lax.optimization_barrier(tuple(arrived) + others)[:3])
        else:
            arrived = after(arrived, *others)
        half = self.kept.shape[1] // 2
        send = (self.kept[:, half:] + arrived[:, half:].astype(jnp.float32)).astype(jnp.bfloat16)
        keep = self.kept[:, :half] + arrived[:, :half].astype(jnp.float32)
        send, self.kept = lax.optimization_barrier((send, keep))
        return send

    def go(self, send, *others):
        if others:
            send = after(send, *others)
        pairs = step_pairs(lax.axis_size("seq"), self.route, self.left.pop(0))
        self.arrived = lax.ppermute(send, "seq", pairs)
        return send

    def finish(self, grad_scale):
        return jnp.transpose((self.kept + self.arrived.astype(jnp.float32)) * grad_scale, (1, 0, 2))


CHUNK = 16
BLOCKS = 4
FREE = pl.CostEstimate(flops=0, bytes_accessed=0, transcendentals=0)


def on_chip(*arrays):
    return [pltpu.with_memory_space_constraint(array, pltpu.VMEM) for array in arrays]


def call(kernel, name, arrays, outs, scratch=(), edges=None, room=8):
    scalars = [] if edges is None else [edges]
    return pl.pallas_call(
        kernel,
        in_specs=[pl.BlockSpec(memory_space=pltpu.SMEM)] * len(scalars)
        + [pl.BlockSpec(memory_space=pltpu.VMEM)] * len(arrays),
        out_specs=[pl.BlockSpec(memory_space=pltpu.VMEM)] * len(outs),
        out_shape=[pltpu.VMEM(shape, dtype) for shape, dtype in outs],
        scratch_shapes=list(scratch),
        compiler_params=pltpu.CompilerParams(vmem_limit_bytes=room * 2**20),
        cost_estimate=FREE,
        name=name,
    )(*scalars, *on_chip(*arrays))


def over_blocks(length, body, unrolled, blocks=BLOCKS):
    rows = length // blocks

    def step(index, carry):
        body(index * rows, rows)
        return carry

    if unrolled:
        for index in range(blocks):
            body(index * rows, rows)
    else:
        lax.fori_loop(0, blocks, step, 0)


def span(first, rows):
    return pl.ds(first if isinstance(first, int) else pl.multiple_of(first, CHUNK), rows)


def inverse_rms(values):
    return lax.rsqrt(jnp.mean(values * values, axis=-1, keepdims=True) + 1e-06)


def cumulative_of(normed):
    return 0.5 * (1.0 + lax.erf(normed * 0.7071067811865476))


def activate(first, rel_ref, active_ref):
    for start in range(0, rel_ref.shape[0], CHUNK):
        values = rel_ref[start : start + CHUNK].astype(jnp.float32)
        normed = values * inverse_rms(values)
        active_ref[span(first + start, CHUNK)] = (normed * cumulative_of(normed)).astype(jnp.bfloat16)


def inside(edge_ref, first, rows):
    row = first + lax.broadcasted_iota(jnp.int32, (rows, 1), 0)
    return (row >= edge_ref[0]) & (row < edge_ref[1])


def join_kernel(first_ref, second_ref, out_ref):
    rows = first_ref.shape[1]
    out_ref[:, :rows] = first_ref[...]
    out_ref[:, rows:] = second_ref[...]


def join_rows(first, second):
    taps, rows, channels = first.shape
    if rows % 16:
        return jnp.concatenate([first, second], axis=1)
    shape = (taps, 2 * rows, channels)
    return call(join_kernel, "join_rows", [first, second], [(shape, first.dtype)], room=4)[0]


def active_kernel(
    odd_ref, layer_in_ref, grad_ref, inner_ref, outer_ref, turn_ref, next_turn_ref,
    wide_in_ref, wide_grad_ref, active_ref, rel_ref, grad_rel_ref, *, offset
):
    length = layer_in_ref.shape[0]
    halo = inner_ref.shape[0] // 2
    odd = odd_ref[0] == 1
    for index, (wide_ref, own_ref) in enumerate(((wide_in_ref, layer_in_ref), (wide_grad_ref, grad_ref))):
        rows = slice(index * halo, (index + 1) * halo)
        wide_ref[:halo] = jnp.where(odd, inner_ref[rows], outer_ref[rows])
        wide_ref[halo : halo + length] = own_ref[...]
        wide_ref[halo + length :] = jnp.where(odd, outer_ref[rows], inner_ref[rows])

    def own_block(first, rows):
        rel_ref[span(first, rows)] = jnp.dot(
            wide_in_ref[span(first, rows)], turn_ref[...], preferred_element_type=jnp.float32
        ).astype(jnp.bfloat16)
        activate(first, rel_ref.at[span(first, rows)], active_ref)

    def grad_block(first, rows):
        grad_rel_ref[span(first, rows)] = jnp.dot(
            wide_grad_ref[span(offset + first, rows)],
            next_turn_ref[...],
            preferred_element_type=jnp.float32,
        ).astype(jnp.bfloat16)

    over_blocks(wide_in_ref.shape[0], own_block, False)
    over_blocks(grad_rel_ref.shape[0], grad_block, False)


def first_active(odd, layer_in, grad, inner, outer, turn, next_turn, offset, back_rows):
    length, channels = layer_in.shape
    rows = length + inner.shape[0]
    wide = ((rows, channels), jnp.bfloat16)
    return call(
        lambda *refs: active_kernel(*refs, offset=offset),
        "first_active",
        [layer_in, grad, inner, outer, turn, next_turn],
        [wide, wide, wide, wide, ((back_rows, channels), jnp.bfloat16)],
        (),
        odd,
        room=6,
    )


def layer_kernel(edge_ref, *refs, spacing, offset, follow):
    pieces, (active_ref, layer_in_ref, *refs) = refs[:4], refs[4:]
    if follow:
        turn_ref, out_ref, rel_ref, next_ref, weight = refs
    else:
        out_ref, weight = refs
    length, channels = out_ref.shape
    size = channels // 4
    for tap in range(3):
        for index, piece in enumerate(pieces):
            first = tap * channels + index * size
            weight[first : first + size] = piece[tap]

    def block(first, rows):
        windows = [active_ref[span(first + tap * spacing, rows)] for tap in range(3)]
        mixed = jnp.dot(
            jnp.concatenate(windows, axis=1), weight[...], preferred_element_type=jnp.float32
        )
        out = layer_in_ref[span(offset + first, rows)].astype(jnp.float32) + mixed
        if follow:
            out = jnp.where(inside(edge_ref, first, rows), out, 0.0)
        out = out.astype(jnp.bfloat16)
        out_ref[span(first, rows)] = out
        if follow:
            rel_ref[span(first, rows)] = jnp.dot(
                out, turn_ref[...], preferred_element_type=jnp.float32
            ).astype(jnp.bfloat16)
            activate(first, rel_ref.at[span(first, rows)], next_ref)

    over_blocks(length, block, follow, 6 if follow else BLOCKS)


def layer(edges, pieces, active, layer_in, offset, length, spacing, turn=None):
    channels = active.shape[1]
    follow = turn is not None
    shape = (length, channels)
    outs = [(shape, jnp.bfloat16)]
    if follow:
        outs += [(shape, jnp.bfloat16)] * 2
    return call(
        lambda *refs: layer_kernel(*refs, spacing=spacing, offset=offset, follow=follow),
        "layer",
        [*pieces, active, layer_in] + ([turn] if follow else []),
        outs,
        [pltpu.VMEM((3 * channels, channels), jnp.bfloat16)],
        edges,
    )


def weight_kernel(active_ref, grad_ref, *outs, spacing, offset, halo, side):
    channels = active_ref.shape[1]
    length = grad_ref.shape[0] - 2 * halo
    half = channels // 2
    turned = active_ref[offset : offset + length, side * half : (side + 1) * half].T
    for tap in range(3):
        first = halo + (1 - tap) * spacing
        term = jnp.dot(
            turned, grad_ref[first : first + length], preferred_element_type=jnp.float32
        )
        if len(outs) == 3:
            outs[tap][...] = term.astype(jnp.bfloat16)
        else:
            outs[0][tap] = term


def weight_term(active, offset, grad_wide, side, spacing, halo):
    channels = active.shape[1]
    half = channels // 2
    if side == 0:
        outs = [((3, half, channels), jnp.float32)]
    else:
        outs = [((half, channels), jnp.bfloat16)] * 3
    out = call(
        lambda *refs: weight_kernel(*refs, spacing=spacing, offset=offset, halo=halo, side=side),
        "weight_term",
        [active, grad_wide],
        outs,
    )
    return out[0] if side == 0 else out


def pass_kernel(edge_ref, *refs, spacing, offset, unrolled):
    pieces, refs = refs[:4], refs[4:]
    grad_ref, layer_in_ref, turn_ref, *refs = refs
    grad_rel_ref, out_ref, rel_ref, weight, act_grad = refs if unrolled else refs[-1:] + refs[:-1]
    length, channels = out_ref.shape
    size = channels // 4
    for tap in range(3):
        for index, piece in enumerate(pieces):
            weight[index * size : (index + 1) * size, tap * channels : (tap + 1) * channels] = piece[tap]

    def block(first, rows):
        windows = [grad_ref[span(first + (2 - tap) * spacing, rows)] for tap in range(3)]
        act_grad[...] = lax.dot_general(
            jnp.concatenate(windows, axis=1),
            weight[...],
            (((1,), (1,)), ((), ())),
            preferred_element_type=jnp.float32,
        )
        if not unrolled:
            grad_rel_ref[...] = jnp.dot(
                grad_ref[span(first + spacing, rows)], turn_ref[...], preferred_element_type=jnp.float32
            ).astype(jnp.bfloat16)
        for start in range(0, rows, CHUNK):
            values = layer_in_ref[span(offset + first + start, CHUNK)].astype(jnp.float32)
            inv_rms = inverse_rms(values)
            normed = values * inv_rms
            slope = (
                cumulative_of(normed)
                + normed * jnp.exp(-0.5 * normed * normed) * 0.3989422804014327
            )
            norm_grad = act_grad[start : start + CHUNK] * slope
            passed = grad_rel_ref[span(first + start if unrolled else start, CHUNK)].astype(jnp.float32) + inv_rms * (
                norm_grad - normed * jnp.mean(norm_grad * normed, axis=-1, keepdims=True)
            )
            passed = jnp.where(inside(edge_ref, first + start, CHUNK), passed, 0.0)
            rel_ref[start : start + CHUNK] = passed.astype(jnp.bfloat16)
        out_ref[span(first, rows)] = lax.dot_general(
            rel_ref[...], turn_ref[...], (((1,), (1,)), ((), ())), preferred_element_type=jnp.float32
        ).astype(jnp.bfloat16)

    over_blocks(length, block, unrolled)


def pass_down(edges, pieces, grad_pad, layer_in, offset, turn, spacing, grad_rel=None):
    length = grad_pad.shape[0] - 2 * spacing
    channels = layer_in.shape[1]
    unrolled = grad_rel is not None
    shape = (length, channels)
    return call(
        lambda *refs: pass_kernel(*refs, spacing=spacing, offset=offset, unrolled=unrolled),
        "pass_down",
        [*pieces, grad_pad, layer_in, turn] + ([grad_rel] if unrolled else []),
        [(shape, jnp.bfloat16)],
        [
            pltpu.VMEM((length // BLOCKS, channels), jnp.bfloat16),
            pltpu.VMEM((channels, 3 * channels), jnp.bfloat16),
            pltpu.VMEM((length // BLOCKS, channels), jnp.float32),
        ]
        + [pltpu.VMEM((length // BLOCKS, channels), jnp.bfloat16)] * (not unrolled),
        edges,
    )[0]


def per_device(inputs, weight_one, weight_two, cotangent):
    count = lax.axis_size("seq")
    me = lax.axis_index("seq")
    length, channels = inputs.shape
    grad_scale = 1.0 / math.sqrt(length * count)
    block = weight_one.shape[0]
    routes = routes_of(count)
    turn_one = one_hot(count, routes[0], block)
    turn_two = one_hot(count, routes[1], block)

    back_rows = length + 2 * DILATION_A
    hidden_rows = length + 2 * DILATION_B

    def edges_of(rows, halo):
        first = jnp.where(me > 0, 0, halo)
        last = jnp.where(me < count - 1, rows, rows - halo)
        return jnp.stack([first, last]).astype(jnp.int32)

    odd = (me & 1) == 1
    scalars = lax.optimization_barrier(
        (
            edges_of(hidden_rows, DILATION_B),
            edges_of(back_rows, DILATION_A),
            edges_of(length, 0),
            odd.astype(jnp.int32).reshape(1),
            turn_one,
            turn_two,
        )
    )
    hidden_edges, back_edges, own_edges, odd_flag, turn_one, turn_two = scalars

    one, two = Gather(weight_one, routes[0]), Gather(weight_two, routes[1])

    def gather_both(*others):
        joined = two.join(*others)
        joined = one.join(joined)
        one.send()
        two.send()
        return joined

    one.send()
    edges_low = jnp.concatenate([inputs[:HALO], cotangent[:HALO]])
    edges_high = jnp.concatenate([inputs[length - HALO :], cotangent[length - HALO :]])
    inner = jnp.where(odd, edges_low, edges_high)
    outer = jnp.where(odd, edges_high, edges_low)
    joined = one.join(inner, outer, *scalars)
    one.send()
    two.held = after(two.held, joined)
    two.send()
    across = [(i, i + 1) for i in range(1, count - 1, 2)] + [(i + 1, i) for i in range(1, count - 1, 2)]
    inner = lax.ppermute(after(inner, joined), "seq", core_pairs(count))
    outer = lax.ppermute(after(outer, joined), "seq", across)
    joined = one.join()
    one.send()
    joined = two.join(joined, inner, outer)
    two.send()
    for _ in range(one.steps - 3):
        joined = gather_both()
    wide_in, wide_cot, active_one, rel_one, cot_rel = first_active(
        odd_flag, inputs, cotangent, inner, outer, turn_one, turn_two, DILATION_B, back_rows
    )
    joined = gather_both(cot_rel)
    full_one = one.full()

    hidden, rel_two, active_two = layer(
        hidden_edges,
        full_one,
        after(active_one, joined),
        wide_in,
        DILATION_A,
        hidden_rows,
        DILATION_A,
        turn_two,
    )
    send_two = weight_term(active_two, DILATION_B, wide_cot, 1, DILATION_B, HALO)
    scatter_two = Scatter(send_two, routes[1])
    joined = two.join(*send_two)
    two.send()
    full_two = two.full()
    scatter_two.keep(
        weight_term(active_two, DILATION_B, after(wide_cot, joined), 0, DILATION_B, HALO)
    )
    sent = scatter_two.add()

    wide_grad = pass_down(
        back_edges,
        full_two,
        after(wide_cot, sent),
        rel_two,
        DILATION_B - DILATION_A,
        turn_two,
        DILATION_B,
        cot_rel,
    )

    send_one = weight_term(active_one, HALO, wide_grad, 1, DILATION_A, DILATION_A)
    scatter_one = Scatter(send_one, routes[0])
    keep_one = weight_term(active_one, HALO, after(wide_grad, *send_one), 0, DILATION_A, DILATION_A)
    scatter_one.keep(keep_one)
    send = scatter_two.total(keep_one)
    sent = scatter_one.add(send)
    sent = scatter_two.go(send, sent)
    input_grad = pass_down(
        own_edges,
        full_one,
        after(wide_grad, sent),
        rel_one,
        HALO,
        turn_one,
        DILATION_A,
    )
    sent = scatter_one.add(input_grad)
    sent = scatter_two.add(sent)
    (outputs,) = layer(
        own_edges,
        full_two,
        after(active_two, sent),
        hidden,
        DILATION_B,
        length,
        DILATION_B,
    )
    rest = [outputs]
    while scatter_one.left:
        if scatter_two.left:
            rest = [scatter_two.add(*rest)]
        rest = [scatter_one.add(*rest)]
    grad_one = scatter_one.finish(grad_scale)
    grad_two = scatter_two.finish(grad_scale)
    return (outputs, input_grad, grad_one, grad_two)


def solution(mesh):
    in_specs = (P("seq", None), P("seq", None, None), P("seq", None, None), P("seq", None))
    out_specs = (P("seq", None), P("seq", None), P("seq", None, None), P("seq", None, None))
    return jax.shard_map(
        per_device, mesh=mesh, in_specs=in_specs, out_specs=out_specs, check_vma=False
    )
```
